32 devices in a mesh: dp: 4 (over y, x), seq: 8 (over z, core).
Axes of the slice: x: 2, y: 2, z: 4, core: 2. Of those that a mesh axis runs over, the one named last changes fastest.
Arguments:
- tokens_in: bfloat16 [8, 4096, 512], P('dp', 'seq'), may hold values from -6 to 6
- cotangent: bfloat16 [8, 4096, 512], P('dp', 'seq'), may hold values from -6 to 6
- lengths: int32 [8], P('dp'), may hold values from 1024 to 4096, as said below
- experts_top: int32 [8, 4096, 2], P('dp', 'seq'), may hold values from 0 to 7, all different within a row
- gains: float32 [2, 512], replicated, may hold values from 0.5 to 1.5
- router: float32 [512, 8], replicated, may hold values from -0.25 to 0.25
- query_w: float32 [8, 512, 64], replicated, may hold values from -0.625 to 0.625
- key_value_w: float32 [2, 512, 64], replicated, may hold values from -0.25 to 0.25
- out_w: float32 [8, 64, 512], replicated, may hold values from -2 to 2
- up_w: float32 [512, 2048], replicated, may hold values from -0.25 to 0.25
- down_w: float32 [2048, 512], replicated, may hold values from -0.125 to 0.125
- gains_mom: float32 [2, 512], replicated, may hold values from -1536 to 1536
- router_mom: float32 [512, 8], replicated, may hold values from -4096 to 4096
- query_mom: float32 [8, 512, 64], replicated, may hold values from -1024 to 1024
- key_value_mom: float32 [2, 512, 64], replicated, may hold values from -2048 to 2048
- out_mom: float32 [8, 64, 512], replicated, may hold values from -160 to 160
- up_mom: float32 [512, 2048], replicated, may hold values from -320 to 320
- down_mom: float32 [2048, 512], replicated, may hold values from -640 to 640
Outputs:
- layer_out: bfloat16 [8, 4096, 512], P('dp', 'seq')
- input_grad: bfloat16 [8, 4096, 512], P('dp', 'seq')
- gains_new: float32 [2, 512], replicated
- gains_mom_new: float32 [2, 512], replicated
- router_new: float32 [512, 8], replicated
- router_mom_new: float32 [512, 8], replicated
- query_new: float32 [8, 512, 64], replicated
- query_mom_new: float32 [8, 512, 64], replicated
- key_value_new: float32 [2, 512, 64], replicated
- key_value_mom_new: float32 [2, 512, 64], replicated
- out_new: float32 [8, 64, 512], replicated
- out_mom_new: float32 [8, 64, 512], replicated
- up_new: float32 [512, 2048], replicated
- up_mom_new: float32 [512, 2048], replicated
- down_new: float32 [2048, 512], replicated
- down_mom_new: float32 [2048, 512], replicated
The draws below stay inside these ranges and needn't reach their ends.
Inputs may be any that keep to these rules, and one draw needn't show every extreme that they name: `lengths`: in every group of 2 sequences of one index of dp, one, chosen by the seed, has all 4096 positions valid. `experts_top`: the 2 experts of a token differ.
All inputs are finite; a program needn't handle non-finite values.
Results may differ from the reference program's by a relative error of at most 0.017.
Values may be sent and summed in bfloat16 or wider, within the bound.
No kernel may reach another device: no remote copies, remote signals or barrier semaphores. Data moves between devices by JAX's collectives and lax.ppermute only.
A program may use at most 192 MiB of HBM per device.

```python
import math
import jax
import jax.numpy as jnp
from jax import lax

D = 512
FF = 2048
EXPERTS = 8
HD = 64
TOPK = 2
SEQ_DEV = 2
L = 4096
BATCH = 8
TOKENS = 32768


def draw_lengths(key, part):
    key = jax.random.fold_in(key, 11)
    pair_key, pick_key = jax.random.split(key)
    shorter = jax.random.randint(pair_key, (BATCH,), L // 4, L + 1)
    groups = BATCH // SEQ_DEV
    full_slot = jax.random.randint(pick_key, (groups,), 0, SEQ_DEV)
    slot_index = jnp.arange(BATCH, dtype=jnp.int32) % SEQ_DEV
    full_here = slot_index == jnp.repeat(full_slot, SEQ_DEV)
    return jnp.where(full_here, L, shorter).astype(jnp.int32)


def block_scale(stream_key, extent, cuts, smallest, largest):
    def one(position, parts):
        heights = jax.random.uniform(jax.random.fold_in(jax.random.fold_in(stream_key, 6), position), (parts,), jnp.float32, smallest / len(cuts), largest / len(cuts))
        return jnp.repeat(jnp.exp(heights), extent[position] // parts).reshape((-1,) + (1,) * (len(extent) - position - 1))

    factor_of = one(*cuts[0])
    for cut in cuts[1:]:
        factor_of = factor_of * one(*cut)
    return factor_of


def choose_distinct(key, rows, count, top, lift):
    ranking = jax.random.permutation(jax.random.fold_in(key, 1), count)
    favour = ranking
    for power in range(3):
        favour = favour * favour // count
    favour = favour * lift // count
    tickets = jax.random.randint(jax.random.fold_in(key, 2), (rows, count), 0, 4096) + favour
    sure = jax.random.permutation(jax.random.fold_in(key, 3), rows)[jnp.arange(count) % rows]
    tickets = jnp.where(jnp.arange(rows)[:, None] == sure[None, :], 1 << 14, tickets)
    merit = tickets * count + jnp.arange(count)
    return lax.top_k(merit.astype(jnp.int32), top)[1].astype(jnp.int32)


def gaussian(key, shape, scale, limit, cuts=(), kind=jnp.bfloat16):
    gain = block_scale(key, shape, cuts, -0.22, 0.18) if cuts else 1.0
    values = jax.random.normal(key, shape, jnp.float32) * scale * gain
    return jnp.minimum(jnp.maximum(values, -limit), limit).astype(kind)


def setup_inputs(seed: int = 0) -> dict:
    key_of = jax.random.split(jax.random.key(seed), 19)
    tokens_in = gaussian(key_of[0], (BATCH, L, D), 1.0, 6.0, ((0, 4), (1, 8)))
    cotangent = gaussian(key_of[1], (BATCH, L, D), 1.0, 6.0, ((0, 4), (1, 8)))
    lengths = draw_lengths(jax.random.fold_in(key_of[18], 71), 0)
    experts_top = choose_distinct(key_of[3], BATCH * L, EXPERTS, TOPK, 2048).reshape((BATCH, L, TOPK))
    gains = jnp.clip(1.0 + 0.1 * jax.random.normal(key_of[4], (2, D), jnp.float32), 0.5, 1.5)
    router = gaussian(key_of[5], (D, EXPERTS), D ** -0.5, 0.25, (), jnp.float32)
    query_w = gaussian(key_of[6], (EXPERTS, D, HD), (D // 6) ** -0.5, 0.625, (), jnp.float32)
    key_value_w = gaussian(key_of[7], (2, D, HD), D ** -0.5, 0.25, (), jnp.float32)
    out_w = gaussian(key_of[8], (EXPERTS, HD, D), (HD // 8) ** -0.5, 2.0, (), jnp.float32)
    up_w = gaussian(key_of[9], (D, FF), D ** -0.5, 0.25, (), jnp.float32)
    down_w = gaussian(key_of[10], (FF, D), FF ** -0.5, 0.125, (), jnp.float32)
    gains_mom = gaussian(key_of[11], (2, D), (1.5 * TOKENS ** 0.5), 1536.0, (), jnp.float32)
    router_mom = gaussian(key_of[12], (D, EXPERTS), (4.0 * TOKENS ** 0.5), 4096.0, (), jnp.float32)
    query_mom = gaussian(key_of[13], (EXPERTS, D, HD), (1.0 * TOKENS ** 0.5), 1024.0, (), jnp.float32)
    key_value_mom = gaussian(key_of[14], (2, D, HD), (2.0 * TOKENS ** 0.5), 2048.0, (), jnp.float32)
    out_mom = gaussian(key_of[15], (EXPERTS, HD, D), (0.15 * TOKENS ** 0.5), 160.0, (), jnp.float32)
    up_mom = gaussian(key_of[16], (D, FF), (0.3 * TOKENS ** 0.5), 320.0, (), jnp.float32)
    down_mom = gaussian(key_of[17], (FF, D), (0.6 * TOKENS ** 0.5), 640.0, (), jnp.float32)
    return dict(tokens_in=tokens_in, cotangent=cotangent, lengths=lengths, experts_top=experts_top, gains=gains, router=router, query_w=query_w, key_value_w=key_value_w, out_w=out_w, up_w=up_w, down_w=down_w, gains_mom=gains_mom, router_mom=router_mom, query_mom=query_mom, key_value_mom=key_value_mom, out_mom=out_mom, up_mom=up_mom, down_mom=down_mom)


@jax.custom_vjp
def low(v):
    return lax.optimization_barrier(v.astype(jnp.bfloat16)).astype(jnp.float32)

@jax.custom_vjp
def low_back(v):
    return v

def low_keep(v):
    return (low(v), None)

def low_pass(kept, grad):
    return (grad,)

def back_keep(v):
    return (v, None)

def back_low(kept, grad):
    return (low(grad),)
low.defvjp(low_keep, low_pass)
low_back.defvjp(back_keep, back_low)
EPSILON = 1e-05
HIGHEST = lax.Precision.HIGHEST
NEWTON_A = 3.4445
NEWTON_B = -4.775
NEWTON_C = 2.0315
STEP_RATE = 0.3
GAIN_RATE = 0.1
MOMENT_DECAY = 0.5

def layer_norm(values_in):
    average = lax.optimization_barrier(jnp.mean(values_in, axis=-1, keepdims=True))
    centred = values_in - average
    return centred * lax.rsqrt(lax.optimization_barrier(jnp.mean(centred * centred, axis=-1, keepdims=True)) + EPSILON)

def attend_block(queries, keys, values, key_mask):
    scores = low_back(HD ** (-0.5) * jnp.einsum('qjh,kh->qjk', queries, keys, precision=HIGHEST))
    scores = jnp.where(key_mask[None, None, :], scores, -1e+30)
    row_max = lax.optimization_barrier(jnp.max(scores, axis=-1, keepdims=True))
    exponent = jnp.exp(scores - row_max)
    row_sum = lax.optimization_barrier(jnp.sum(exponent, axis=-1, keepdims=True))
    weighted = low_back(jnp.einsum('qjk,kh->qjh', low(exponent), values, precision=HIGHEST))
    return weighted / row_sum

def attend_sequence(operands):
    queries, keys, values, key_mask = operands
    block_rows = min(512, L)
    blocks = queries.reshape(L // block_rows, block_rows, TOPK, HD)

    def one_block(query_block):
        return attend_block(query_block, keys, values, key_mask)
    attended = lax.map(jax.checkpoint(one_block), blocks)
    return attended.reshape(L, TOPK, HD)

def forward(inputs, gains, router, query_w, key_value_w, out_w, up_w, down_w, chosen, key_mask):
    normed = layer_norm(inputs)
    hidden = low(normed * gains[0])
    logits = low_back(jnp.einsum('bld,de->ble', hidden, low(router), precision=HIGHEST))
    picked = lax.optimization_barrier(jnp.sum(chosen * logits[:, :, None, :], axis=-1))
    gating = jax.nn.softmax(picked, axis=-1)
    query_all = jnp.einsum('bld,edh->bleh', hidden, low(query_w), precision=HIGHEST)
    queries = low(low_back(jnp.einsum('blje,bleh->bljh', chosen, query_all, precision=HIGHEST)))
    key_value = low(low_back(jnp.einsum('bld,cdh->cblh', hidden, low(key_value_w), precision=HIGHEST)))
    attended = lax.map(attend_sequence, (queries, key_value[0], key_value[1], key_mask))
    spread = low(jnp.einsum('blje,blj,bljh->bleh', chosen, gating, attended, precision=HIGHEST))
    branch = low_back(jnp.einsum('bleh,ehd->bld', spread, low(out_w), precision=HIGHEST))
    middle = inputs + branch
    hidden_two = low(layer_norm(middle) * gains[1])
    inner = low_back(jnp.einsum('bld,df->blf', hidden_two, low(up_w), precision=HIGHEST))
    activated = low(jax.nn.gelu(inner))
    return middle + jnp.einsum('blf,fd->bld', activated, low(down_w), precision=HIGHEST)

def orthogonalize(stacked):
    tall = stacked.shape[-2] > stacked.shape[-1]
    matrix = jnp.swapaxes(stacked, -1, -2) if tall else stacked
    matrix = matrix / (jnp.sqrt(lax.optimization_barrier(jnp.sum(matrix * matrix, axis=(-2, -1), keepdims=True))) + 1e-07)
    for _ in range(5):
        gram = jnp.einsum('nij,nkj->nik', matrix, matrix, precision=HIGHEST)
        poly = NEWTON_B * gram + NEWTON_C * jnp.einsum('nij,njk->nik', gram, gram, precision=HIGHEST)
        matrix = NEWTON_A * matrix + jnp.einsum('nij,njk->nik', poly, matrix, precision=HIGHEST)
    return jnp.swapaxes(matrix, -1, -2) if tall else matrix

def renew_matrices(weight, moment, gradient):
    renewed = MOMENT_DECAY * moment + gradient
    solved = orthogonalize(renewed)
    shortest = min(weight.shape[-2], weight.shape[-1])
    norm_scale = jnp.sqrt(lax.optimization_barrier(jnp.sum(weight * weight, axis=(-2, -1), keepdims=True))) / math.sqrt(shortest)
    return (weight - STEP_RATE * norm_scale * solved, renewed)

def reference(tokens_in, cotangent, lengths, experts_top, gains, router, query_w, key_value_w, out_w, up_w, down_w, gains_mom, router_mom, query_mom, key_value_mom, out_mom, up_mom, down_mom):
    positions = jnp.arange(L, dtype=jnp.int32)
    key_mask = positions[None, :] < lengths[:, None]
    chosen = (experts_top[..., None] == jnp.arange(EXPERTS, dtype=jnp.int32)).astype(jnp.float32)

    def layer(inputs, gain_pair, router_in, query_in, pair_in, out_in, up_in, down_in):
        return forward(inputs, gain_pair, router_in, query_in, pair_in, out_in, up_in, down_in, chosen, key_mask)
    operands = (tokens_in.astype(jnp.float32), gains, router, query_w, key_value_w, out_w, up_w, down_w)
    result, pull = jax.vjp(layer, *operands)
    returned = cotangent.astype(jnp.float32) * key_mask[..., None].astype(jnp.float32)
    gradients = pull(returned)
    gains_mom_new = MOMENT_DECAY * gains_mom + gradients[1]
    gains_new = gains - GAIN_RATE / math.sqrt(TOKENS) * gains_mom_new
    router_new, router_mom_new = renew_matrices(router[None], router_mom[None], gradients[2][None])
    query_new, query_mom_new = renew_matrices(query_w, query_mom, gradients[3])
    pair_new, pair_mom_new = renew_matrices(key_value_w, key_value_mom, gradients[4])
    out_new, out_mom_new = renew_matrices(out_w, out_mom, gradients[5])
    up_new, up_mom_new = renew_matrices(up_w[None], up_mom[None], gradients[6][None])
    down_new, down_mom_new = renew_matrices(down_w[None], down_mom[None], gradients[7][None])
    return (result.astype(jnp.bfloat16), gradients[0].astype(jnp.bfloat16), gains_new, gains_mom_new, router_new[0], router_mom_new[0], query_new, query_mom_new, pair_new, pair_mom_new, out_new, out_mom_new, up_new[0], up_mom_new[0], down_new[0], down_mom_new[0])
```

```python
import functools
import math

import jax
import jax.numpy as jnp
from jax import lax
from jax.experimental import pallas as pl
from jax.experimental.pallas import tpu as pltpu
from jax.sharding import PartitionSpec as P

EPSILON = 1e-05
NEWTON_A = 3.4445
NEWTON_B = -4.775
NEWTON_C = 2.0315
STEP_RATE = 0.3
GAIN_RATE = 0.1
MOMENT_DECAY = 0.5
LOG2E = math.log2(math.e)
GELU_A = math.sqrt(2.0 / math.pi)
GELU_B = 0.044715
MASKED = -1e30
MIB = 1 << 20

F32 = jnp.float32
BF16 = jnp.bfloat16

NN = (((1,), (0,)), ((), ()))
NT = (((1,), (1,)), ((), ()))
TN = (((0,), (0,)), ((), ()))


def dot(left, right, dims=NN):
    return lax.dot_general(left, right, dims, preferred_element_type=F32)


def params(mib=58):
    return pltpu.CompilerParams(vmem_limit_bytes=mib * MIB)


def cost(giga, mib=4, exps=0):
    return pl.CostEstimate(flops=int(giga * 1e7), bytes_accessed=mib * 4096, transcendentals=exps)


def whole():
    return pl.BlockSpec(memory_space=pltpu.VMEM)


def scalars():
    return pl.BlockSpec(memory_space=pltpu.SMEM)


def normalize(values_in):
    average = jnp.mean(values_in, axis=-1, keepdims=True)
    centred = values_in - average
    inv_std = lax.rsqrt(jnp.mean(centred * centred, axis=-1, keepdims=True) + EPSILON)
    return centred * inv_std, inv_std


def norm_back(normed, inv_std, d_normed):
    first = jnp.mean(d_normed, axis=-1, keepdims=True)
    second = jnp.mean(d_normed * normed, axis=-1, keepdims=True)
    return inv_std * (d_normed - first - normed * second)


def split_rows(row, count):
    index = lax.broadcasted_iota(jnp.int32, (count, row.shape[1]), 0)
    block = jnp.zeros((count, row.shape[1]), F32)
    for term in range(3):
        part = row.astype(BF16).astype(F32)
        block = jnp.where(index == term, part, block)
        row = row - part
    return block


def pick_expert(row, stacked, experts):
    size = stacked.shape[0] // experts
    total = jnp.where(row == 0, stacked[:size], 0.0)
    for expert in range(1, experts):
        total = total + jnp.where(row == expert, stacked[expert * size : (expert + 1) * size], 0.0)
    return total


def place_experts(rows, blocks, experts):
    pieces = []
    for expert in range(experts):
        piece = jnp.where(rows[0] == expert, blocks[0], 0.0)
        for row, block in zip(rows[1:], blocks[1:]):
            piece = piece + jnp.where(row == expert, block, 0.0)
        pieces.append(piece)
    return jnp.concatenate(pieces, axis=0)


def project_kernel(
    tok_ref, exp_ref, gain_ref, wq_ref, wkv_ref, wr_ref, hid_ref, kv_ref, q_ref, scaled_ref, gat_ref
):
    experts = wr_ref.shape[0]
    shard = tok_ref.shape[1]
    head = wkv_ref.shape[0] // 2
    ones = (lax.broadcasted_iota(jnp.int32, (2 * head, shard), 0) == 0).astype(F32)
    normed, _ = normalize(tok_ref[0].astype(F32))
    hidden = (normed * gain_ref[0:1, :]).astype(BF16)
    hid_ref[0] = hidden
    kv_ref[0] = dot(hidden, wkv_ref[...].astype(BF16), NT).astype(BF16)
    query_all = dot(wq_ref[...].astype(BF16), hidden, NT)
    logits = dot(wr_ref[...].astype(BF16), hidden, NT)
    chosen = exp_ref[0]
    choices = chosen.shape[0]
    picked = []
    for j in range(choices):
        row = chosen[j : j + 1, :]
        cols = slice(j * shard, (j + 1) * shard)
        query = pick_expert(row, query_all, experts).astype(BF16).astype(F32)
        exponent = query * (head**-0.5 * LOG2E)
        high = exponent.astype(BF16).astype(F32)
        q_ref[0, :, cols] = jnp.concatenate([high, exponent - high, ones], axis=0).astype(BF16)
        scaled_ref[0, :, cols] = (query * head**-0.5).astype(BF16)
        picked.append(pick_expert(row, logits, experts))
    top = functools.reduce(jnp.maximum, picked)
    raised = [jnp.exp(value - top) for value in picked]
    total = functools.reduce(jnp.add, raised)
    for j in range(choices):
        gat_ref[0, :, j * shard : (j + 1) * shard] = raised[j] / total


def project(tokens, chosen, gains, wq, wkv, wr):
    batch, shard, width = tokens.shape
    choices = chosen.shape[1]
    head = wkv.shape[0] // 2
    columns = choices * shard
    full = lambda array: pl.BlockSpec(array.shape, lambda b: (0,) * array.ndim)
    each = lambda *shape: pl.BlockSpec((1,) + shape, lambda b: (b, 0, 0))
    return pl.pallas_call(
        project_kernel,
        grid=(batch,),
        in_specs=[each(shard, width), each(choices, shard), full(gains), full(wq), full(wkv), full(wr)],
        out_specs=[
            each(shard, width),
            each(shard, 2 * head),
            each(4 * head, columns),
            each(head, columns),
            each(1, columns),
        ],
        out_shape=[
            jax.ShapeDtypeStruct((batch, shard, width), BF16),
            jax.ShapeDtypeStruct((batch, shard, 2 * head), BF16),
            jax.ShapeDtypeStruct((batch, 4 * head, columns), BF16),
            jax.ShapeDtypeStruct((batch, head, columns), BF16),
            jax.ShapeDtypeStruct((batch, 1, columns), F32),
        ],
        compiler_params=params(),
        cost_estimate=cost(4, 4),
        name="project",
    )(tokens, chosen, gains, wq, wkv, wr)


def spread_keys(block, count):
    rows, pair = block.shape
    head = pair // 2
    lane = lax.broadcasted_iota(jnp.int32, block.shape, 1)
    position = lax.broadcasted_iota(jnp.int32, block.shape, 0)
    twice = jnp.where(lane < head, block, pltpu.roll(block, head, 1))
    mask = jnp.where(position >= count, MASKED, 0.0)
    extra = jnp.where(lane == 0, mask, jnp.where(lane <= 3, 1.0, 0.0))
    return jnp.concatenate([twice, extra], axis=1).astype(BF16)


def attend_kernel(*refs, base, chunks, first, last, part):
    refs = list(refs)
    tab_ref, q_ref = refs[:2]
    kv_refs = refs[2 : 2 + chunks]
    rest = refs[2 + chunks :]
    if first:
        state = None
    else:
        state, rest = rest[:2], rest[2:]
    max_ref, acc_ref = rest[-2:]
    rest = rest[:-2]
    columns = q_ref.shape[2]
    head = q_ref.shape[1] // 4
    length = tab_ref[pl.program_id(0)]
    if first:
        max_ref[...] = jnp.full(max_ref.shape, MASKED, F32)
        acc_ref[...] = jnp.zeros_like(acc_ref)
    else:
        max_ref[...] = state[0][0]
        acc_ref[...] = state[1][0]
    parts = [slice(at, at + part) for at in range(0, columns, part)]
    for index, kv_ref in enumerate(kv_refs):
        count = length - tab_ref[base + index]

        @pl.when(count > 0)
        def _(kv_ref=kv_ref, count=count):
            block = kv_ref[0].astype(F32)
            keys = spread_keys(block, count)
            extra = acc_ref.shape[0] - head
            values = jnp.concatenate(
                [block.T[head:].astype(BF16), jnp.ones((extra, block.shape[0]), BF16)], axis=0
            )
            before = [max_ref[:, cols] for cols in parts]
            sums = [acc_ref[:, cols] for cols in parts]
            scores = [dot(keys, q_ref[0, :, cols]) for cols in parts]
            after = [
                jnp.maximum(old, jnp.max(score, axis=0, keepdims=True))
                for old, score in zip(before, scores)
            ]
            expos = [jnp.exp2(score - new).astype(BF16) for score, new in zip(scores, after)]
            shrinks = [jnp.exp2(old - new) for old, new in zip(before, after)]
            sums = [total * shrink + dot(values, expo) for total, shrink, expo in zip(sums, shrinks, expos)]
            for cols, new, total in zip(parts, after, sums):
                max_ref[:, cols] = new
                acc_ref[:, cols] = total

    if last:
        att_ref, sum_ref, back_ref = rest
        row_sum = acc_ref[head : head + 1, :]
        sum_ref[0] = row_sum
        att_ref[0] = acc_ref[:head, :] / row_sum
        back_ref[0, : 2 * head, :] = q_ref[0, : 2 * head, :]
        ones = (lax.broadcasted_iota(jnp.int32, (1, columns), 0) == 0).astype(F32)
        tail = jnp.concatenate([ones, split_rows(-max_ref[...], 2 * head - 1)], axis=0)
        back_ref[0, 2 * head :, :] = tail.astype(BF16)
    else:
        rest[0][0] = max_ref[...]
        rest[1][0] = acc_ref[...]


def attend(table, base, queries, chunks, state, last, part=256):
    batch, deep, columns = queries.shape
    head = deep // 4
    tall = head + 16
    each = lambda *shape: pl.BlockSpec((1,) + shape, lambda b: (b, 0, 0))
    row = jax.ShapeDtypeStruct((batch, 1, columns), F32)
    if last:
        out_specs = [each(head, columns), each(1, columns), each(deep, columns)]
        out_shape = [jax.ShapeDtypeStruct((batch, head, columns), F32), row]
        out_shape += [jax.ShapeDtypeStruct(queries.shape, BF16)]
    else:
        out_specs = [each(1, columns), each(tall, columns)]
        out_shape = [row, jax.ShapeDtypeStruct((batch, tall, columns), F32)]
    return pl.pallas_call(
        functools.partial(
            attend_kernel, base=base, chunks=len(chunks), first=state is None, last=last, part=part
        ),
        grid=(batch,),
        in_specs=[scalars(), each(deep, columns)]
        + [each(*chunk.shape[1:]) for chunk in chunks]
        + ([] if state is None else [each(1, columns), each(tall, columns)]),
        out_specs=out_specs,
        out_shape=out_shape,
        scratch_shapes=[pltpu.VMEM((1, columns), F32), pltpu.VMEM((tall, columns), F32)],
        compiler_params=params(),
        cost_estimate=cost(7, 1),
        name="attend",
    )(table, queries, *chunks, *([] if state is None else state))


def attend_back_kernel(*refs, base, sends, keeps, first, part):
    refs = list(refs)
    chunks = sends + keeps
    tab_ref, q_ref, scaled_ref, dw_ref = refs[:4]
    kv_refs = refs[4 : 4 + chunks]
    rest = refs[4 + chunks :]
    if first:
        before = None
    else:
        before, rest = rest[0], rest[1:]
    dq_ref, rest = rest[0], rest[1:]
    targets = [rest[0].at[index, 0] for index in range(sends)]
    targets += [ref.at[0] for ref in rest[len(rest) - keeps :]]
    columns = q_ref.shape[2]
    head = q_ref.shape[1] // 4
    length = tab_ref[pl.program_id(0)]
    dq_ref[0] = jnp.zeros((head, columns), F32) if first else before[0]
    parts = [slice(at, at + part) for at in range(0, columns, part)]
    for index, kv_ref in enumerate(kv_refs):
        count = length - tab_ref[base + index]
        target = targets[index]

        @pl.when(count > 0)
        def _(kv_ref=kv_ref, count=count, target=target):
            block = kv_ref[0].astype(F32)
            keys = spread_keys(block, count)
            lane = lax.broadcasted_iota(jnp.int32, block.shape, 1)
            values = jnp.where(lane < head, jnp.where(lane < 3, 1.0, 0.0), block).astype(BF16)
            keys_t = block.T[:head].astype(BF16)

            def products(cols):
                return dot(keys, q_ref[0, :, cols]), dot(values, dw_ref[0, :, cols])

            d_keys = jnp.zeros((head, block.shape[0]), F32)
            d_values = jnp.zeros((head, block.shape[0]), F32)
            ahead = products(parts[0])
            for p, cols in enumerate(parts):
                scores, d_expo = ahead
                if p + 1 < len(parts):
                    ahead = products(parts[p + 1])
                expo = jnp.exp2(scores)
                d_scores = (expo * d_expo).astype(BF16)
                dq_ref[0, :, cols] += dot(keys_t, d_scores)
                d_keys = d_keys + dot(scaled_ref[0, :, cols], d_scores, NT)
                d_values = d_values + dot(dw_ref[0, head:, cols], expo.astype(BF16), NT)
            target[:head, :] = d_keys.astype(BF16)
            target[head:, :] = d_values.astype(BF16)

        @pl.when(count <= 0)
        def _(target=target):
            target[...] = jnp.zeros(target.shape, BF16)


def attend_back(table, base, queries, scaled, d_weighted, sends, keeps, d_query, part=256):
    batch, deep, columns = queries.shape
    head, pair = deep // 4, deep // 2
    chunks = sends + keeps
    size = chunks[0].shape[1]
    each = lambda *shape: pl.BlockSpec((1,) + shape, lambda b: (b, 0, 0))
    stack = pl.BlockSpec((len(sends), 1, pair, size), lambda b: (0, b, 0, 0))
    stacked = [jax.ShapeDtypeStruct((len(sends), batch, pair, size), BF16)] if sends else []
    outs = pl.pallas_call(
        functools.partial(
            attend_back_kernel,
            base=base,
            sends=len(sends),
            keeps=len(keeps),
            first=d_query is None,
            part=part,
        ),
        grid=(batch,),
        in_specs=[
            scalars(),
            each(deep, columns),
            each(head, columns),
            each(pair, columns),
        ]
        + [each(size, pair)] * len(chunks)
        + ([] if d_query is None else [each(head, columns)]),
        out_specs=[each(head, columns)] + [stack] * len(stacked) + [each(pair, size)] * len(keeps),
        out_shape=[jax.ShapeDtypeStruct((batch, head, columns), F32)]
        + stacked
        + [jax.ShapeDtypeStruct((batch, pair, size), BF16)] * len(keeps),
        compiler_params=params(),
        cost_estimate=cost(8, 2),
        name="attend_back",
    )(
        table,
        queries,
        scaled,
        d_weighted,
        *chunks,
        *([] if d_query is None else [d_query]),
    )
    return outs[0], outs[1] if sends else None, outs[len(outs) - len(keeps) :]


def middle_kernel(
    len_ref,
    tok_ref,
    cot_ref,
    exp_ref,
    att_ref,
    gat_ref,
    sum_ref,
    gain_ref,
    wo_in_ref,
    up_ref,
    down_ref,
    out_ref,
    dmid_ref,
    dw_ref,
    dlog_ref,
    keep_ref,
    send_ref,
    gout_ref,
    ggain_ref,
    act_ref,
    din_ref,
    hid_ref,
    dres_ref,
    low_ref,
    spread_ref,
    wo_ref,
    *,
    batch,
    experts,
    chunk,
):
    step = pl.program_id(0)
    _, shard, width = tok_ref.shape
    hidden_units = up_ref.shape[1]
    choices = exp_ref.shape[1]

    @pl.when(step == 0)
    def _():
        wo_ref[...] = wo_in_ref[...].astype(BF16)

    @pl.when(step < batch)
    def _():
        rows = pl.ds(pl.multiple_of(step * shard, shard), shard)
        length = len_ref[step]
        offset = len_ref[batch]
        chosen = exp_ref[0]
        each = [slice(j * shard, (j + 1) * shard) for j in range(choices)]
        which = [chosen[j : j + 1, :] for j in range(choices)]
        gating = [gat_ref[0, :, cols] for cols in each]
        attended = [att_ref[0, :, cols] for cols in each]
        spread = place_experts(which, [g * a for g, a in zip(gating, attended)], experts).astype(BF16)
        spread_ref[:, rows] = spread
        middle = tok_ref[0].astype(F32) + dot(spread, wo_ref[...], TN)
        normed, inv_std = normalize(middle)
        gain = gain_ref[1:2, :]
        hidden = (normed * gain).astype(BF16)
        hid_ref[rows, :] = hidden
        position = offset + lax.broadcasted_iota(jnp.int32, (shard, width), 0)
        d_result = jnp.where(position < length, cot_ref[0].astype(F32), 0.0)
        d_result_low = d_result.astype(BF16)
        dres_ref[rows, :] = d_result_low
        result = middle
        d_hidden = jnp.zeros((shard, width), F32)
        for c in range(hidden_units // chunk):
            cols = slice(c * chunk, (c + 1) * chunk)
            inner = dot(hidden, up_ref[:, cols])
            square = inner * inner
            half = 0.5 * jnp.tanh(inner * (GELU_A + (GELU_A * GELU_B) * square)) + 0.5
            activated = (inner * half).astype(BF16)
            slope = half + (2.0 * inner) * (half - half * half) * (
                GELU_A + (3.0 * GELU_A * GELU_B) * square
            )
            act_ref[rows, cols] = activated
            result = result + dot(activated, down_ref[cols, :])
            d_inner = (dot(d_result_low, down_ref[cols, :], NT) * slope).astype(BF16)
            din_ref[rows, cols] = d_inner
            d_hidden = d_hidden + dot(d_inner, up_ref[:, cols], NT)
        out_ref[0] = result.astype(BF16)
        own_gain = jnp.sum(normed * d_hidden, axis=0, keepdims=True)

        @pl.when(step == 0)
        def _():
            ggain_ref[...] = own_gain

        @pl.when(step > 0)
        def _():
            ggain_ref[...] += own_gain

        d_middle = d_result + norm_back(normed, inv_std, d_hidden * gain)
        dmid_ref[0] = d_middle
        d_middle_low = d_middle.astype(BF16)
        low_ref[rows, :] = d_middle_low
        d_spread = dot(wo_ref[...], d_middle_low, NT)
        d_gating = []
        for j in range(choices):
            selected = pick_expert(which[j], d_spread, experts)
            d_gating.append(jnp.sum(selected * attended[j], axis=0, keepdims=True))
            share = 1.0 / sum_ref[0, :, each[j]]
            d_weighted = selected * (gating[j] * share)
            d_total = split_rows(-(gating[j] * d_gating[j]) * share, d_weighted.shape[0])
            dw_ref[0, :, each[j]] = jnp.concatenate([d_total, d_weighted], axis=0).astype(BF16)
        mixed = functools.reduce(jnp.add, [g * d for g, d in zip(gating, d_gating)])
        expert_row = lax.broadcasted_iota(jnp.int32, (experts, shard), 0)
        d_logits = jnp.zeros((experts, shard), F32)
        for j in range(choices):
            d_logits = d_logits + jnp.where(expert_row == which[j], gating[j] * (d_gating[j] - mixed), 0.0)
        dlog_ref[0] = d_logits.astype(BF16)

    @pl.when(step >= batch)
    def _():
        late = keep_ref.shape[1]
        cols = pl.ds(pl.multiple_of((step - batch) * late, late), late)
        grad_up = dot(hid_ref[...], din_ref[:, cols], TN)
        grad_down = dot(dres_ref[...], act_ref[:, cols], TN)
        first = len_ref[batch + 1] == 0
        keep_ref[...] = jnp.where(first, grad_up, grad_down).astype(BF16)
        send_ref[...] = jnp.where(first, grad_down, grad_up).astype(BF16)

    @pl.when(step == batch)
    def _():
        gout_ref[...] = dot(spread_ref[...], low_ref[...]).astype(BF16)


def middle(limits, tokens, cotangent, chosen, attended, gating, row_sum, gains, wo, up, down, experts):
    batch, shard, width = tokens.shape
    _, head, columns = attended.shape
    choices = chosen.shape[1]
    hidden_units = up.shape[1]
    chunk = 512
    parts = hidden_units // chunk
    full = lambda *shape: pl.BlockSpec(shape, lambda i: (0,) * len(shape))
    each = lambda *shape: pl.BlockSpec((1,) + shape, lambda i: (jnp.minimum(i, batch - 1), 0, 0))
    once = lambda *shape: pl.BlockSpec(
        shape, lambda i: (0,) * len(shape), pipeline_mode=pl.Buffered(1)
    )
    late = lambda i: jnp.maximum(i - batch, 0)
    spread_rows = wo.shape[0]
    total = batch * shard
    return pl.pallas_call(
        functools.partial(middle_kernel, batch=batch, experts=experts, chunk=chunk),
        grid=(batch + parts,),
        in_specs=[
            scalars(),
            each(shard, width),
            each(shard, width),
            each(choices, shard),
            each(head, columns),
            each(1, columns),
            each(1, columns),
            full(*gains.shape),
            once(*wo.shape),
            once(*up.shape),
            once(*down.shape),
        ],
        out_specs=[
            each(shard, width),
            each(shard, width),
            each(2 * head, columns),
            each(experts, shard),
            pl.BlockSpec((width, chunk), lambda i: (0, late(i))),
            pl.BlockSpec((width, chunk), lambda i: (0, late(i))),
            full(*wo.shape),
            full(1, width),
        ],
        out_shape=[
            jax.ShapeDtypeStruct((batch, shard, width), BF16),
            jax.ShapeDtypeStruct((batch, shard, width), F32),
            jax.ShapeDtypeStruct((batch, 2 * head, columns), BF16),
            jax.ShapeDtypeStruct((batch, experts, shard), BF16),
            jax.ShapeDtypeStruct((width, hidden_units), BF16),
            jax.ShapeDtypeStruct((width, hidden_units), BF16),
            jax.ShapeDtypeStruct(wo.shape, BF16),
            jax.ShapeDtypeStruct((1, width), F32),
        ],
        scratch_shapes=[
            pltpu.VMEM((total, hidden_units), BF16),
            pltpu.VMEM((total, hidden_units), BF16),
            pltpu.VMEM((total, width), BF16),
            pltpu.VMEM((total, width), BF16),
            pltpu.VMEM((total, width), BF16),
            pltpu.VMEM((spread_rows, total), BF16),
            pltpu.VMEM(wo.shape, BF16),
        ],
        compiler_params=params(),
        cost_estimate=cost(28, 20),
        name="middle",
    )(limits, tokens, cotangent, chosen, attended, gating, row_sum, gains, wo, up, down)


def query_grad_kernel(hid_ref, dq_ref, exp_ref, dlog_ref, wq_ref, wr_ref, gq_ref, gr_ref, dhid_ref, sum_ref):
    experts = wr_ref.shape[0]
    shard = hid_ref.shape[1]
    head = dq_ref.shape[1]
    choices = exp_ref.shape[1]
    step = pl.program_id(0)
    hidden = hid_ref[0]
    chosen = exp_ref[0]
    which = [chosen[j : j + 1, :] for j in range(choices)]
    blocks = [dq_ref[0, :, j * shard : (j + 1) * shard] * head**-0.5 for j in range(choices)]
    d_query_all = place_experts(which, blocks, experts).astype(BF16)
    d_logits = dlog_ref[0]
    own_query = dot(d_query_all, hidden)
    own_router = dot(d_logits, hidden)

    @pl.when(step == 0)
    def _():
        sum_ref[...] = own_query
        gr_ref[...] = own_router

    @pl.when(step > 0)
    def _():
        sum_ref[...] += own_query
        gr_ref[...] += own_router

    gq_ref[...] = sum_ref[...].astype(BF16)

    dhid_ref[0] = dot(d_query_all, wq_ref[...].astype(BF16), TN) + dot(
        d_logits, wr_ref[...].astype(BF16), TN
    )


def query_grad(hidden, d_query, chosen, d_logits, wq, wr):
    batch, shard, width = hidden.shape
    _, head, columns = d_query.shape
    choices = chosen.shape[1]
    experts = wr.shape[0]
    full = lambda *shape: pl.BlockSpec(shape, lambda b: (0,) * len(shape))
    each = lambda *shape: pl.BlockSpec((1,) + shape, lambda b: (b, 0, 0))
    return pl.pallas_call(
        query_grad_kernel,
        grid=(batch,),
        in_specs=[
            each(shard, width),
            each(head, columns),
            each(choices, shard),
            each(experts, shard),
            full(*wq.shape),
            full(*wr.shape),
        ],
        out_specs=[full(*wq.shape), full(*wr.shape), each(shard, width)],
        out_shape=[
            jax.ShapeDtypeStruct(wq.shape, BF16),
            jax.ShapeDtypeStruct(wr.shape, F32),
            jax.ShapeDtypeStruct((batch, shard, width), F32),
        ],
        scratch_shapes=[pltpu.VMEM(wq.shape, F32)],
        compiler_params=params(),
        cost_estimate=cost(2, 6),
        name="query_grad",
    )(hidden, d_query, chosen, d_logits, wq, wr)


def input_grad_kernel(
    tok_ref,
    hid_ref,
    dpair_ref,
    dhid_ref,
    dmid_ref,
    gain_ref,
    wkv_ref,
    query_ref,
    out_ref,
    router_ref,
    two_ref,
    gin_ref,
    tail_ref,
    gkv_ref,
    one_ref,
):
    step = pl.program_id(0)
    normed, inv_std = normalize(tok_ref[0].astype(F32))
    d_pair = dpair_ref[0]
    d_hidden = dhid_ref[0] + dot(d_pair, wkv_ref[...].astype(BF16), TN)
    own_pair = dot(d_pair, hid_ref[0])
    own_gain = jnp.sum(normed * d_hidden, axis=0, keepdims=True)

    @pl.when(step == 0)
    def _():
        gkv_ref[...] = own_pair
        one_ref[...] = own_gain

    @pl.when(step > 0)
    def _():
        gkv_ref[...] += own_pair
        one_ref[...] += own_gain

    d_inputs = dmid_ref[0] + norm_back(normed, inv_std, d_hidden * gain_ref[0:1, :])
    gin_ref[0] = d_inputs.astype(BF16)
    query_rows, width = query_ref.shape
    head_rows = query_rows + out_ref.shape[0]
    used = head_rows + gkv_ref.shape[0] + router_ref.shape[0] + 2
    blank = jnp.zeros((tail_ref.shape[0] - used, width), F32)
    small = [gkv_ref[...], router_ref[...], one_ref[...], two_ref[...], blank]
    tail_ref[:query_rows, :] = query_ref[...]
    tail_ref[query_rows:head_rows, :] = out_ref[...]
    tail_ref[head_rows:, :] = jnp.concatenate(small, axis=0).astype(BF16)


def input_grad(
    tokens, hidden, d_pair, d_hidden, d_middle, gains, wkv, grad_query, grad_out, grad_router, grad_gain_two
):
    batch, shard, width = tokens.shape
    pair = wkv.shape[0]
    rows = -(-(grad_query.shape[0] + grad_out.shape[0] + pair + grad_router.shape[0] + 2) // 64) * 64
    full = lambda *shape: pl.BlockSpec(shape, lambda b: (0,) * len(shape))
    each = lambda *shape: pl.BlockSpec((1,) + shape, lambda b: (b, 0, 0))
    return pl.pallas_call(
        input_grad_kernel,
        grid=(batch,),
        in_specs=[
            each(shard, width),
            each(shard, width),
            each(pair, shard),
            each(shard, width),
            each(shard, width),
            full(*gains.shape),
            full(*wkv.shape),
            full(*grad_query.shape),
            full(*grad_out.shape),
            full(*grad_router.shape),
            full(*grad_gain_two.shape),
        ],
        out_specs=[each(shard, width), full(rows, width)],
        out_shape=[
            jax.ShapeDtypeStruct((batch, shard, width), BF16),
            jax.ShapeDtypeStruct((rows, width), BF16),
        ],
        scratch_shapes=[pltpu.VMEM(wkv.shape, F32), pltpu.VMEM((1, width), F32)],
        compiler_params=params(),
        cost_estimate=cost(2, 9),
        name="input_grad",
    )(tokens, hidden, d_pair, d_hidden, d_middle, gains, wkv, grad_query, grad_out, grad_router, grad_gain_two)


def square_fine(matrix):
    high = matrix.astype(BF16)
    rest = (matrix - high.astype(F32)).astype(BF16)
    cross = dot(high, rest)
    return dot(high, high) + (cross + cross.T)


def mirrored(left, bottom):
    half = bottom.shape[0]
    right = jnp.concatenate([left[half:].T, bottom], axis=0)
    return jnp.concatenate([left, right], axis=1)


def gram_of(low):
    half = low.shape[0] // 2
    return mirrored(dot(low, low[:half], NT), dot(low[half:], low[half:], NT))


def square_of(gram):
    half = gram.shape[0] // 2
    high = gram.astype(BF16)
    rest = (gram - high.astype(F32)).astype(BF16)
    cross = dot(high, rest)
    return mirrored(dot(high, high[:, :half]), dot(high[half:], high[:, half:])) + (cross + cross.T)


def muon_kernel(core_ref, up_ref, down_ref, grad_in_ref, solved_ref, x_ref, low_ref, turn_ref, grad_ref, sems):
    rows, cols = x_ref.shape
    fetch = pltpu.make_async_copy(grad_in_ref, grad_ref, sems.at[0])
    fetch.start()

    @pl.when(core_ref[0] == 0)
    def _():
        copy = pltpu.make_async_copy(up_ref, x_ref, sems.at[1])
        copy.start()
        copy.wait()

    @pl.when(core_ref[0] != 0)
    def _():
        pieces = range(0, cols, rows)
        copies = [
            pltpu.make_async_copy(
                down_ref.at[pl.ds(at, rows), :], turn_ref.at[pl.ds(at, rows), :], sems.at[2 + index]
            )
            for index, at in enumerate(pieces)
        ]
        for copy in copies:
            copy.start()
        for copy, at in zip(copies, pieces):
            copy.wait()
            x_ref[:, at : at + rows] = turn_ref[at : at + rows, :].T

    fetch.wait()

    renewed = MOMENT_DECAY * x_ref[...] + grad_ref[:, :cols].astype(F32)
    inverse = 1.0 / (jnp.sqrt(jnp.sum(renewed * renewed)) + 1e-07)
    first = renewed * inverse
    x_ref[...] = first
    low_ref[...] = first.astype(BF16)

    def iterate(_, carry):
        low = low_ref[...]
        gram = gram_of(low)
        poly = (NEWTON_B * gram + NEWTON_C * square_of(gram)).astype(BF16)
        following = NEWTON_A * x_ref[...] + dot(poly, low)
        x_ref[...] = following
        low_ref[...] = following.astype(BF16)
        return carry

    lax.fori_loop(0, 5, iterate, 0)
    solved_ref[...] = low_ref[...]


def muon(core_ref, up_mom, down_mom, grad):
    anywhere = pl.BlockSpec(memory_space=pl.ANY)
    return pl.pallas_call(
        muon_kernel,
        in_specs=[scalars(), anywhere, anywhere, anywhere],
        out_specs=whole(),
        out_shape=jax.ShapeDtypeStruct(up_mom.shape, BF16),
        scratch_shapes=[
            pltpu.VMEM(up_mom.shape, F32),
            pltpu.VMEM(up_mom.shape, BF16),
            pltpu.VMEM(down_mom.shape, F32),
            pltpu.VMEM(grad.shape, BF16),
            pltpu.SemaphoreType.DMA((2 + max(down_mom.shape) // min(down_mom.shape),)),
        ],
        compiler_params=params(),
        cost_estimate=cost(25, 8),
        name="muon",
    )(core_ref, up_mom, down_mom, grad)


def prepare_kernel(up_ref, down_ref, up_low_ref, down_low_ref, up_square_ref, down_square_ref):
    for ref, low_ref, square_ref in (
        (up_ref, up_low_ref, up_square_ref),
        (down_ref, down_low_ref, down_square_ref),
    ):
        weight = ref[...]
        low_ref[...] = weight.astype(BF16)
        total = jnp.sum(jnp.sum(weight * weight, axis=0, keepdims=True), axis=1, keepdims=True)

        @pl.when(pl.program_id(0) == 0)
        def _(square_ref=square_ref, total=total):
            square_ref[...] = total

        @pl.when(pl.program_id(0) > 0)
        def _(square_ref=square_ref, total=total):
            square_ref[...] += total


def prepare(up, down, steps=4):
    rows, cols = up.shape
    one = pl.BlockSpec((1, 1), lambda i: (0, 0))
    flat = pl.BlockSpec((rows // steps, cols), lambda i: (i, 0))
    turned = pl.BlockSpec((cols // steps, rows), lambda i: (i, 0))
    return pl.pallas_call(
        prepare_kernel,
        grid=(steps,),
        in_specs=[flat, turned],
        out_specs=[flat, turned, one, one],
        out_shape=[
            jax.ShapeDtypeStruct(up.shape, BF16),
            jax.ShapeDtypeStruct(down.shape, BF16),
            jax.ShapeDtypeStruct((1, 1), F32),
            jax.ShapeDtypeStruct((1, 1), F32),
        ],
        compiler_params=params(),
        cost_estimate=cost(1, 12),
        name="prepare",
    )(up, down)


def blend_block(first, square_refs, refs, rank):
    up_ref, down_ref, own_rows, other_rows, own_cols, other_cols, up_out, down_out = refs
    for ref, out, one, two, turn in (
        (up_ref, up_out, own_rows, other_rows, False),
        (down_ref, down_out, other_cols, own_cols, True),
    ):
        change = jnp.where(first, one[...].astype(F32), two[...].astype(F32))
        change = change.T if turn else change
        if square_refs:
            step = jnp.sqrt(square_refs[1 if turn else 0][...]) * (STEP_RATE / math.sqrt(rank))
            out[...] = ref[...] - step * change
        else:
            out[...] = MOMENT_DECAY * ref[...] + change


def blend_specs(up, down, steps):
    rows, cols = up.shape
    flat = pl.BlockSpec((rows // steps, cols), lambda i, core: (i, 0))
    turned = pl.BlockSpec((cols // steps, rows), lambda i, core: (i, 0))

    def wanted(i, core, turn):
        return jnp.where(core[0] == turn, i, 0)

    row_specs = [
        pl.BlockSpec((rows // steps, cols), lambda i, core, turn=turn: (wanted(i, core, turn), 0)) for turn in (0, 1)
    ]
    col_specs = [
        pl.BlockSpec((rows, cols // steps), lambda i, core, turn=turn: (0, wanted(i, core, turn))) for turn in (1, 0)
    ]
    return [flat, turned] + row_specs + col_specs, [flat, turned]


def by_block(values, sizes, finish):
    pieces = []
    at = 0
    for size in sizes:
        piece = values[at : at + size]
        total = jnp.sum(jnp.sum(piece * piece, axis=1, keepdims=True), axis=0, keepdims=True)
        pieces.append(jnp.broadcast_to(finish(total, size), (size, 1)))
        at += size
    return jnp.concatenate(pieces, axis=0)


def block_ids(sizes, axis):
    index = lax.broadcasted_iota(jnp.int32, (sum(sizes), sum(sizes)), axis)
    ids = jnp.zeros(index.shape, jnp.int32)
    at = 0
    for size in sizes[:-1]:
        at += size
        ids = ids + (index >= at).astype(jnp.int32)
    return ids


def solve_packs(step, sizes, x_ref, renew, weights_of, store):
    @pl.when(step == 0)
    def _():
        for index, moment in enumerate(renew()):
            x_ref[index] = moment * by_block(moment, sizes, lambda total, _: 1.0 / (jnp.sqrt(total) + 1e-07))

    @pl.when((step >= 1) & (step <= 5))
    def _():
        same = block_ids(sizes, 0) == block_ids(sizes, 1)
        matrices = [x_ref[index] for index in range(x_ref.shape[0])]
        lows = [matrix.astype(BF16) for matrix in matrices]
        grams = [jnp.where(same, dot(low, low, NT), 0.0) for low in lows]
        squares = [square_fine(gram) for gram in grams]
        polys = [(NEWTON_B * g + NEWTON_C * q).astype(BF16) for g, q in zip(grams, squares)]
        for index, (matrix, poly, low) in enumerate(zip(matrices, polys, lows)):
            x_ref[index] = NEWTON_A * matrix + dot(poly, low)

    @pl.when(step == 6)
    def _():
        fresh = []
        for index, (weight, ranks) in enumerate(weights_of()):
            factors = iter([STEP_RATE / math.sqrt(min(weight.shape[1], rank)) for rank in ranks])
            scale = by_block(weight, sizes, lambda total, _: jnp.sqrt(total) * next(factors))
            fresh.append(weight - scale * x_ref[index])
        store(fresh)


STEPS = 8


def renew_kernel(core_ref, *refs):
    blend_block(core_ref[0] == 0, [], refs, min(refs[2].shape))


def renew(core_ref, up_mom, down_mom, own, other):
    ins, outs = blend_specs(up_mom, down_mom, STEPS)
    return pl.pallas_call(
        renew_kernel,
        grid_spec=pltpu.PrefetchScalarGridSpec(num_scalar_prefetch=1, grid=(STEPS,), in_specs=ins, out_specs=outs),
        out_shape=[jax.ShapeDtypeStruct(array.shape, F32) for array in (up_mom, down_mom)],
        compiler_params=params(),
        cost_estimate=cost(1, 20),
        name="renew",
    )(core_ref, up_mom, down_mom, own, other, own, other)


def move_kernel(core_ref, *refs, head, gain_rate, rank):
    square_refs = refs[:2]
    blend_refs = refs[2:8] + refs[19:21]
    wq_ref, wo_ref, wkv_ref, wr_ref, gain_ref, mq_ref, mo_ref, mkv_ref, mr_ref, mgain_ref, tail_ref = refs[8:19]
    wq_out, wo_out, wkv_out, wr_out, gain_out, mq_out, mo_out, mkv_out, mr_out, mgain_out, x_ref = refs[21:]
    sizes = (head,) * 4
    rows = sum(sizes)
    query_rows, pair, experts = wq_ref.shape[0], wkv_ref.shape[0], wr_ref.shape[0]
    head_rows = query_rows + wo_ref.shape[0]
    places = [
        (weight, moment, target, slice(at, at + rows))
        for weight, moment, target in ((wq_ref, mq_out, wq_out), (wo_ref, mo_out, wo_out))
        for at in range(0, weight.shape[0], rows)
    ]
    blank = jnp.zeros((rows - pair - experts, wkv_ref.shape[1]), F32)

    def renewed():
        mq_out[...] = MOMENT_DECAY * mq_ref[...] + tail_ref[:query_rows, :].astype(F32)
        mo_out[...] = MOMENT_DECAY * mo_ref[...] + tail_ref[query_rows:head_rows, :].astype(F32)
        small = tail_ref[head_rows:, :].astype(F32)
        mkv_out[...] = MOMENT_DECAY * mkv_ref[...] + small[:pair]
        mr_out[...] = MOMENT_DECAY * mr_ref[...] + small[pair : pair + experts]
        gain_moment = MOMENT_DECAY * mgain_ref[...] + small[pair + experts : pair + experts + 2]
        mgain_out[...] = gain_moment
        gain_out[...] = gain_ref[...] - gain_rate * gain_moment
        last = jnp.concatenate([mkv_out[...], mr_out[...], blank], axis=0)
        return [moment[at, :] for _, moment, _, at in places] + [last]

    def weights_of():
        last = jnp.concatenate([wkv_ref[...], wr_ref[...], blank], axis=0)
        return [(weight[at, :], sizes) for weight, _, _, at in places] + [(last, (head, head, experts, head))]

    def store(fresh):
        for (_, _, target, at), value in zip(places, fresh):
            target[at, :] = value
        wkv_out[...] = fresh[-1][:pair]
        wr_out[...] = fresh[-1][pair : pair + experts]

    solve_packs(pl.program_id(0), sizes, x_ref, renewed, weights_of, store)
    blend_block(core_ref[0] == 0, square_refs, blend_refs, rank)


def move_and_tail(core_ref, squares, up, down, own, other, weights, moments, tail, head, gain_rate):
    ins, outs = blend_specs(up, down, STEPS)
    one = pl.BlockSpec((1, 1), lambda i, core: (0, 0))
    full = lambda array: pl.BlockSpec(array.shape, lambda i, core: (0, 0))
    arrays = weights + moments
    rows = 4 * head
    return pl.pallas_call(
        functools.partial(move_kernel, head=head, gain_rate=gain_rate, rank=min(up.shape)),
        grid_spec=pltpu.PrefetchScalarGridSpec(
            num_scalar_prefetch=1,
            grid=(STEPS,),
            in_specs=[one, one] + ins + [full(array) for array in arrays + [tail]],
            out_specs=outs + [full(array) for array in arrays],
            scratch_shapes=[pltpu.VMEM(((weights[0].shape[0] + weights[1].shape[0]) // rows + 1, rows, up.shape[0]), F32)],
        ),
        out_shape=[jax.ShapeDtypeStruct(array.shape, F32) for array in [up, down] + arrays],
        compiler_params=params(),
        cost_estimate=cost(1, 20),
        name="move_and_tail",
    )(core_ref, *squares, up, down, own, other, own, other, *arrays, tail)


def after(*values):
    return lax.optimization_barrier(values)


class Sums:
    def __init__(self):
        self.planes, self.lines = lax.axis_size("dp"), lax.axis_size("seq")
        plane_bits = range(self.planes.bit_length() - 1)
        self.orders = [[(1 << bit, 0) for bit in bits] for bits in (plane_bits, reversed(plane_bits))]
        self.plane, self.line = lax.axis_index("dp"), lax.axis_index("seq")
        self.table = None

    def send(self, value, pairs):
        if self.table is not None:
            value, self.table = after(value, self.table)
        return lax.ppermute(value, ("dp", "seq"), pairs)

    def exchange(self, value, flips):
        pairs = []
        for plane in range(self.planes):
            for line in range(self.lines):
                flip = flips[line % 2]
                pairs.append((plane * self.lines + line, (plane ^ flip[0]) * self.lines + (line ^ flip[1])))
        return self.send(value, pairs)

    def stages(self):
        return list(zip(*self.orders))

    def upper(self, flips):
        sides = [((self.plane & flip[0]) | (self.line & flip[1])) != 0 for flip in flips]
        return jnp.where(self.line % 2 == 0, sides[0], sides[1])

    def sibling(self, value):
        return self.exchange(value, ((0, 1), (0, 1)))

    def add_up(self, *terms):
        return functools.reduce(jnp.add, [term.astype(F32) for term in terms]).astype(terms[0].dtype)

    def halve(self, rows, upper, flips):
        half = rows.shape[0] // 2
        low, high = rows[:half], rows[half:]
        return self.exchange(jnp.where(upper, low, high), flips), jnp.where(upper, high, low)

    def join(self, rows, arrived, upper):
        return jnp.concatenate([jnp.where(upper, arrived, rows), jnp.where(upper, rows, arrived)], axis=0)

    def to_chip(self, value, mask):
        return self.exchange(value, ((0, 2 * mask), (0, 2 * mask)))


def per_device(
    tokens_in,
    cotangent,
    lengths,
    experts_top,
    gains,
    router,
    query_w,
    key_value_w,
    out_w,
    up_w,
    down_w,
    gains_mom,
    router_mom,
    query_mom,
    key_value_mom,
    out_mom,
    up_mom,
    down_mom,
):
    batch_here, shard_len, width = tokens_in.shape
    experts, _, head = query_w.shape
    seq_devices = lax.axis_size("seq")
    seq_len = shard_len * seq_devices
    token_total = batch_here * lax.axis_size("dp") * seq_len

    def wide(stacked):
        return jnp.swapaxes(stacked, -1, -2).reshape(-1, width)

    def narrow(rows):
        return jnp.swapaxes(rows.reshape(-1, head, width), -1, -2)

    chosen = jnp.swapaxes(experts_top, 1, 2)
    wq, wkv, wr = wide(query_w), wide(key_value_w), router.T
    wo = out_w.reshape(-1, width)
    sums = Sums()
    place = lax.axis_index("seq").astype(jnp.int32)
    core, chip = place % 2, place // 2
    chips = seq_devices // 2
    core_ref = core[None]

    rounds = [
        [away for away in range(chips) if away.bit_count() == bits] for bits in range(chips.bit_length())
    ]
    own_turns = [[(away, core) for away in members] for members in rounds]
    sibling_turns = [[(away, 1 - core) for away in members] for members in rounds]
    forward = [own_turns[0] + sibling_turns[0]] + own_turns[1:] + [[]]
    for turn in range(1, len(rounds)):
        forward[turn + 1] = sibling_turns[turn] + forward[turn + 1]
    last = len(rounds)
    sends_of = [rounds[last - 1 - call] for call in range(last)] + [[]]
    sends_of[last - 2], sends_of[last - 1] = sends_of[last - 2] + rounds[0], []
    keeps_of = [[]] + rounds[::-1]
    backward = [
        [(away, 1 - core) for away in theirs] + [(away, core) for away in ours]
        for theirs, ours in zip(sends_of, keeps_of)
    ]
    bases, starts = [], []
    for group in forward + backward:
        bases.append(batch_here + 2 + len(starts))
        starts += [(2 * (chip ^ away) + which) * shard_len for away, which in group]
    table = jnp.concatenate([lengths, jnp.stack([place * shard_len, core] + starts)])

    hidden, key_value, queries, scaled, gating = project(tokens_in, chosen, gains, wq, wkv, wr)
    sums.table = table
    blocks, siblings = {0: key_value}, {0: sums.sibling(key_value)}
    incoming = [sums.to_chip(key_value, away) for away in rounds[1]]
    state = attend(sums.table, bases[0], queries, [blocks[0], siblings[0]], None, False)
    up_late, state = after(up_w, state)
    up_low, down_low, *squares = prepare(up_late, down_w)
    squares, sums.table = after(squares, sums.table)
    for turn in range(1, len(rounds) + 1):
        group = []
        if turn > 1:
            group += [siblings[away] for away in rounds[turn - 1]]
        if turn < len(rounds):
            incoming, state, sums.table = after(incoming, state, sums.table)
            blocks.update(zip(rounds[turn], incoming))
            group += incoming
            incoming = [
                sums.to_chip(blocks[away & (away - 1)], away & -away)
                for away in (rounds[turn + 1] if turn + 1 < len(rounds) else [])
            ]
            siblings.update((away, sums.sibling(blocks[away])) for away in rounds[turn])
        state = attend(sums.table, bases[turn], queries, group, state, turn == len(rounds))
    attended, row_sum, back_queries = state
    (
        layer_out,
        d_middle,
        d_weighted,
        d_logits,
        keep,
        send,
        grad_out,
        grad_gain_two,
    ) = middle(
        sums.table,
        tokens_in,
        cotangent,
        chosen,
        attended,
        gating,
        row_sum,
        gains,
        wo,
        up_low,
        down_low,
        experts,
    )
    stages = sums.stages()

    def halving(flips):
        def step(arrived):
            return list(sums.halve(sums.add_up(*arrived), sums.upper(flips), flips))

        return step

    def doubling(flips):
        def step(arrived):
            return [arrived[0], sums.exchange(arrived[0], flips)]

        return step

    def joined(flips, step):
        return lambda arrived: step([sums.join(*arrived, sums.upper(flips))])

    stages += [((0, 2 << bit), (0, 2 << bit)) for bit in range(chips.bit_length() - 1)]
    back = stages[::-1]
    ffn_steps = [halving(flips) for flips in stages]
    ffn_steps.append(lambda arrived: doubling(back[0])([sums.add_up(*arrived)]))
    for earlier, flips in zip(back, back[1:]):
        ffn_steps.append(joined(earlier, doubling(flips)))

    ffn = [sums.sibling(send), keep]
    d_query, crossing, arrived = None, {}, {}
    grown = {away: [] for away in range(chips)}
    for call in range(last + 1):
        theirs, ours = sends_of[call], keeps_of[call]
        d_query, d_send, d_keeps = attend_back(
            sums.table,
            bases[last + 1 + call],
            back_queries,
            scaled,
            d_weighted,
            [siblings[away] for away in theirs],
            [blocks[away] for away in ours],
            d_query,
        )
        if call == last:
            break
        d_query, d_send, ffn, crossing, grown = after(d_query, d_send, ffn, crossing, grown)
        if len(ffn_steps) > 5:
            ffn = ffn_steps.pop(0)(ffn)
        arrived.update(crossing)
        crossing = {}
        if theirs:
            exchanged = sums.sibling(d_send)
            crossing = {away: exchanged[i] for i, away in enumerate(theirs)}
        for away, d_keep in zip(ours, d_keeps):
            total = sums.add_up(d_keep, arrived[away], *grown[away])
            grown[away ^ (away & -away)].append(sums.to_chip(total, away & -away))

    sums.table = core_ref
    ffn, d_query = after(ffn, d_query)
    while len(ffn_steps) > 4:
        ffn = ffn_steps.pop(0)(ffn)
    hidden, sums.table = after(hidden, sums.table)
    grad_query, grad_router, d_hidden = query_grad(hidden, d_query, chosen, d_logits, wq, wr)
    sides = [d_keeps[0], arrived[0], *grown[0]]
    ffn, sides, grad_query = after(ffn, sides, grad_query)
    ffn = ffn_steps.pop(0)(ffn)
    d_hidden, sides, sums.table = after(d_hidden, sides, sums.table)
    input_gradient, tail = input_grad(
        tokens_in,
        hidden,
        sums.add_up(*sides),
        d_hidden,
        d_middle,
        gains,
        wkv,
        grad_query,
        grad_out,
        grad_router,
        grad_gain_two,
    )
    second = core == 1
    ffn, tail = after(ffn, tail)
    ffn = ffn_steps.pop(0)(ffn)
    plane_stages = sums.stages()
    plane_back = plane_stages[::-1]
    tail_steps = [halving(flips) for flips in plane_stages]
    tail_steps += [lambda arrived, flips=flips: doubling(flips)([sums.add_up(*arrived)]) for flips in back[::-1][len(plane_back) :]]
    tail_steps.append(lambda arrived: doubling(plane_back[0])([sums.add_up(*arrived)]))
    tail_steps += [joined(earlier, doubling(flips)) for earlier, flips in zip(plane_back, plane_back[1:])]

    def tail_step(tail):
        tail, sums.table = after(tail, sums.table)
        return tail_steps.pop(0)(tail)

    tail = list(sums.halve(tail, second, ((0, 1), (0, 1))))
    tail = tail_step(tail)
    ffn, sums.table = after(ffn, sums.table)
    ffn = ffn_steps.pop(0)(ffn)
    for _ in plane_stages:
        tail = tail_step(tail)
    ffn, sums.table = after(ffn, sums.table)
    ffn = ffn_steps.pop(0)(ffn)
    while len(tail_steps) > 1:
        tail = tail_step(tail)
    ffn, sums.table = after(ffn, sums.table)
    own_ffn = sums.join(*ffn, sums.upper(back[-1]))
    other_ffn = sums.sibling(own_ffn)
    tail = tail_step(tail)
    solved_ffn = muon(sums.table, up_mom, down_mom, own_ffn)
    tail, other_ffn, solved_ffn = after(tail, other_ffn, solved_ffn)
    other_solved = sums.sibling(solved_ffn)
    tail = sums.join(*tail, sums.upper(plane_back[-1]))
    tail = [tail, sums.sibling(tail)]
    up_mom_new, down_mom_new = renew(sums.table, up_mom, down_mom, own_ffn, other_ffn)
    tail, other_solved, up_mom_new = after(tail, other_solved, up_mom_new)
    tail = sums.join(*tail, second)
    (
        up_new,
        down_new,
        query_new,
        out_new,
        pair_new,
        router_new,
        gains_new,
        query_mom_new,
        out_mom_new,
        pair_mom_new,
        router_mom_new,
        gains_mom_new,
    ) = move_and_tail(
        sums.table,
        squares,
        up_w,
        down_w,
        solved_ffn,
        other_solved,
        [wq, wo, wkv, wr, gains],
        [wide(query_mom), out_mom.reshape(-1, width), wide(key_value_mom), router_mom.T, gains_mom],
        tail,
        head,
        GAIN_RATE / math.sqrt(token_total),
    )
    return (
        layer_out,
        input_gradient,
        gains_new,
        gains_mom_new,
        router_new.T,
        router_mom_new.T,
        narrow(query_new),
        narrow(query_mom_new),
        narrow(pair_new),
        narrow(pair_mom_new),
        out_new.reshape(out_w.shape),
        out_mom_new.reshape(out_w.shape),
        up_new,
        up_mom_new,
        down_new,
        down_mom_new,
    )


def solution(mesh):
    split = P("dp", "seq", None)
    return jax.shard_map(
        per_device,
        mesh=mesh,
        in_specs=(split, split, P("dp"), split) + (P(),) * 14,
        out_specs=(split, split) + (P(),) * 14,
        check_vma=False,
    )
```

```python
import functools
import math

import jax
import jax.numpy as jnp
from jax import lax
from jax.experimental import pallas as pl
from jax.experimental.pallas import tpu as pltpu
from jax.sharding import PartitionSpec as P

EPSILON = 1e-05
NEWTON_A = 3.4445
NEWTON_B = -4.775
NEWTON_C = 2.0315
STEP_RATE = 0.3
GAIN_RATE = 0.1
MOMENT_DECAY = 0.5
LOG2E = math.log2(math.e)
GELU_A = math.sqrt(2.0 / math.pi)
GELU_B = 0.044715
MASKED = -1e30
MIB = 1 << 20

F32 = jnp.float32
BF16 = jnp.bfloat16

NN = (((1,), (0,)), ((), ()))
NT = (((1,), (1,)), ((), ()))
TN = (((0,), (0,)), ((), ()))


def dot(left, right, dims=NN):
    return lax.dot_general(left, right, dims, preferred_element_type=F32)


def params(mib=58):
    return pltpu.CompilerParams(vmem_limit_bytes=mib * MIB)


def cost(giga, mib=4, exps=0):
    return pl.CostEstimate(flops=int(giga * 1e7), bytes_accessed=mib * 4096, transcendentals=exps)


def whole():
    return pl.BlockSpec(memory_space=pltpu.VMEM)


def scalars():
    return pl.BlockSpec(memory_space=pltpu.SMEM)


def normalize(values_in):
    average = jnp.mean(values_in, axis=-1, keepdims=True)
    centred = values_in - average
    inv_std = lax.rsqrt(jnp.mean(centred * centred, axis=-1, keepdims=True) + EPSILON)
    return centred * inv_std, inv_std


def norm_back(normed, inv_std, d_normed):
    first = jnp.mean(d_normed, axis=-1, keepdims=True)
    second = jnp.mean(d_normed * normed, axis=-1, keepdims=True)
    return inv_std * (d_normed - first - normed * second)


def split_rows(row, count):
    index = lax.broadcasted_iota(jnp.int32, (count, row.shape[1]), 0)
    block = jnp.zeros((count, row.shape[1]), F32)
    for term in range(3):
        part = row.astype(BF16).astype(F32)
        block = jnp.where(index == term, part, block)
        row = row - part
    return block


def pick_expert(row, stacked, experts):
    size = stacked.shape[0] // experts
    total = jnp.where(row == 0, stacked[:size], 0.0)
    for expert in range(1, experts):
        total = total + jnp.where(row == expert, stacked[expert * size : (expert + 1) * size], 0.0)
    return total


def place_experts(rows, blocks, experts):
    pieces = []
    for expert in range(experts):
        piece = jnp.where(rows[0] == expert, blocks[0], 0.0)
        for row, block in zip(rows[1:], blocks[1:]):
            piece = piece + jnp.where(row == expert, block, 0.0)
        pieces.append(piece)
    return jnp.concatenate(pieces, axis=0)


def project_kernel(
    tok_ref, exp_ref, gain_ref, wq_ref, wkv_ref, wr_ref, hid_ref, kv_ref, q_ref, scaled_ref, gat_ref
):
    experts = wr_ref.shape[0]
    shard = tok_ref.shape[1]
    head = wkv_ref.shape[0] // 2
    ones = (lax.broadcasted_iota(jnp.int32, (2 * head, shard), 0) == 0).astype(F32)
    normed, _ = normalize(tok_ref[0].astype(F32))
    hidden = (normed * gain_ref[0:1, :]).astype(BF16)
    hid_ref[0] = hidden
    kv_ref[0] = dot(hidden, wkv_ref[...].astype(BF16), NT).astype(BF16)
    query_all = dot(wq_ref[...].astype(BF16), hidden, NT)
    logits = dot(wr_ref[...].astype(BF16), hidden, NT)
    chosen = exp_ref[0]
    choices = chosen.shape[0]
    picked = []
    for j in range(choices):
        row = chosen[j : j + 1, :]
        cols = slice(j * shard, (j + 1) * shard)
        query = pick_expert(row, query_all, experts).astype(BF16).astype(F32)
        exponent = query * (head**-0.5 * LOG2E)
        high = exponent.astype(BF16).astype(F32)
        q_ref[0, :, cols] = jnp.concatenate([high, exponent - high, ones], axis=0).astype(BF16)
        scaled_ref[0, :, cols] = (query * head**-0.5).astype(BF16)
        picked.append(pick_expert(row, logits, experts))
    top = functools.reduce(jnp.maximum, picked)
    raised = [jnp.exp(value - top) for value in picked]
    total = functools.reduce(jnp.add, raised)
    for j in range(choices):
        gat_ref[0, :, j * shard : (j + 1) * shard] = raised[j] / total


def project(tokens, chosen, gains, wq, wkv, wr):
    batch, shard, width = tokens.shape
    choices = chosen.shape[1]
    head = wkv.shape[0] // 2
    columns = choices * shard
    full = lambda array: pl.BlockSpec(array.shape, lambda b: (0,) * array.ndim)
    each = lambda *shape: pl.BlockSpec((1,) + shape, lambda b: (b, 0, 0))
    return pl.pallas_call(
        project_kernel,
        grid=(batch,),
        in_specs=[each(shard, width), each(choices, shard), full(gains), full(wq), full(wkv), full(wr)],
        out_specs=[
            each(shard, width),
            each(shard, 2 * head),
            each(4 * head, columns),
            each(head, columns),
            each(1, columns),
        ],
        out_shape=[
            jax.ShapeDtypeStruct((batch, shard, width), BF16),
            jax.ShapeDtypeStruct((batch, shard, 2 * head), BF16),
            jax.ShapeDtypeStruct((batch, 4 * head, columns), BF16),
            jax.ShapeDtypeStruct((batch, head, columns), BF16),
            jax.ShapeDtypeStruct((batch, 1, columns), F32),
        ],
        compiler_params=params(),
        cost_estimate=cost(4, 4),
        name="project",
    )(tokens, chosen, gains, wq, wkv, wr)


def spread_keys(block, count):
    rows, pair = block.shape
    head = pair // 2
    lane = lax.broadcasted_iota(jnp.int32, block.shape, 1)
    position = lax.broadcasted_iota(jnp.int32, block.shape, 0)
    twice = jnp.where(lane < head, block, pltpu.roll(block, head, 1))
    mask = jnp.where(position >= count, MASKED, 0.0)
    extra = jnp.where(lane == 0, mask, jnp.where(lane <= 3, 1.0, 0.0))
    return jnp.concatenate([twice, extra], axis=1).astype(BF16)


def attend_kernel(*refs, base, chunks, first, last, part):
    refs = list(refs)
    tab_ref, q_ref = refs[:2]
    kv_refs = refs[2 : 2 + chunks]
    rest = refs[2 + chunks :]
    if first:
        state = None
    else:
        state, rest = rest[:2], rest[2:]
    max_ref, acc_ref = rest[-2:]
    rest = rest[:-2]
    columns = q_ref.shape[2]
    head = q_ref.shape[1] // 4
    length = tab_ref[pl.program_id(0)]
    if first:
        max_ref[...] = jnp.full(max_ref.shape, MASKED, F32)
        acc_ref[...] = jnp.zeros_like(acc_ref)
    else:
        max_ref[...] = state[0][0]
        acc_ref[...] = state[1][0]
    parts = [slice(at, at + part) for at in range(0, columns, part)]
    for index, kv_ref in enumerate(kv_refs):
        count = length - tab_ref[base + index]

        @pl.when(count > 0)
        def _(kv_ref=kv_ref, count=count):
            block = kv_ref[0].astype(F32)
            keys = spread_keys(block, count)
            extra = acc_ref.shape[0] - head
            values = jnp.concatenate(
                [block.T[head:].astype(BF16), jnp.ones((extra, block.shape[0]), BF16)], axis=0
            )
            before = [max_ref[:, cols] for cols in parts]
            sums = [acc_ref[:, cols] for cols in parts]
            scores = [dot(keys, q_ref[0, :, cols]) for cols in parts]
            after = [
                jnp.maximum(old, jnp.max(score, axis=0, keepdims=True))
                for old, score in zip(before, scores)
            ]
            expos = [jnp.exp2(score - new).astype(BF16) for score, new in zip(scores, after)]
            shrinks = [jnp.exp2(old - new) for old, new in zip(before, after)]
            sums = [total * shrink + dot(values, expo) for total, shrink, expo in zip(sums, shrinks, expos)]
            for cols, new, total in zip(parts, after, sums):
                max_ref[:, cols] = new
                acc_ref[:, cols] = total

    if last:
        att_ref, sum_ref, back_ref = rest
        row_sum = acc_ref[head : head + 1, :]
        sum_ref[0] = row_sum
        att_ref[0] = acc_ref[:head, :] / row_sum
        back_ref[0, : 2 * head, :] = q_ref[0, : 2 * head, :]
        ones = (lax.broadcasted_iota(jnp.int32, (1, columns), 0) == 0).astype(F32)
        tail = jnp.concatenate([ones, split_rows(-max_ref[...], 2 * head - 1)], axis=0)
        back_ref[0, 2 * head :, :] = tail.astype(BF16)
    else:
        rest[0][0] = max_ref[...]
        rest[1][0] = acc_ref[...]


def attend(table, base, queries, chunks, state, last, part=256):
    batch, deep, columns = queries.shape
    head = deep // 4
    tall = head + 16
    each = lambda *shape: pl.BlockSpec((1,) + shape, lambda b: (b, 0, 0))
    row = jax.ShapeDtypeStruct((batch, 1, columns), F32)
    if last:
        out_specs = [each(head, columns), each(1, columns), each(deep, columns)]
        out_shape = [jax.ShapeDtypeStruct((batch, head, columns), F32), row]
        out_shape += [jax.ShapeDtypeStruct(queries.shape, BF16)]
    else:
        out_specs = [each(1, columns), each(tall, columns)]
        out_shape = [row, jax.ShapeDtypeStruct((batch, tall, columns), F32)]
    return pl.pallas_call(
        functools.partial(
            attend_kernel, base=base, chunks=len(chunks), first=state is None, last=last, part=part
        ),
        grid=(batch,),
        in_specs=[scalars(), each(deep, columns)]
        + [each(*chunk.shape[1:]) for chunk in chunks]
        + ([] if state is None else [each(1, columns), each(tall, columns)]),
        out_specs=out_specs,
        out_shape=out_shape,
        scratch_shapes=[pltpu.VMEM((1, columns), F32), pltpu.VMEM((tall, columns), F32)],
        compiler_params=params(),
        cost_estimate=cost(7, 1),
        name="attend",
    )(table, queries, *chunks, *([] if state is None else state))


def attend_back_kernel(*refs, base, sends, keeps, first, part):
    refs = list(refs)
    chunks = sends + keeps
    tab_ref, q_ref, scaled_ref, dw_ref = refs[:4]
    kv_refs = refs[4 : 4 + chunks]
    rest = refs[4 + chunks :]
    if first:
        before = None
    else:
        before, rest = rest[0], rest[1:]
    dq_ref, rest = rest[0], rest[1:]
    targets = [rest[0].at[index, 0] for index in range(sends)]
    targets += [ref.at[0] for ref in rest[len(rest) - keeps :]]
    columns = q_ref.shape[2]
    head = q_ref.shape[1] // 4
    length = tab_ref[pl.program_id(0)]
    dq_ref[0] = jnp.zeros((head, columns), F32) if first else before[0]
    parts = [slice(at, at + part) for at in range(0, columns, part)]
    for index, kv_ref in enumerate(kv_refs):
        count = length - tab_ref[base + index]
        target = targets[index]

        @pl.when(count > 0)
        def _(kv_ref=kv_ref, count=count, target=target):
            block = kv_ref[0].astype(F32)
            keys = spread_keys(block, count)
            lane = lax.broadcasted_iota(jnp.int32, block.shape, 1)
            values = jnp.where(lane < head, jnp.where(lane < 3, 1.0, 0.0), block).astype(BF16)
            keys_t = block.T[:head].astype(BF16)

            def products(cols):
                return dot(keys, q_ref[0, :, cols]), dot(values, dw_ref[0, :, cols])

            d_keys = jnp.zeros((head, block.shape[0]), F32)
            d_values = jnp.zeros((head, block.shape[0]), F32)
            ahead = products(parts[0])
            for p, cols in enumerate(parts):
                scores, d_expo = ahead
                if p + 1 < len(parts):
                    ahead = products(parts[p + 1])
                expo = jnp.exp2(scores)
                d_scores = (expo * d_expo).astype(BF16)
                dq_ref[0, :, cols] += dot(keys_t, d_scores)
                d_keys = d_keys + dot(scaled_ref[0, :, cols], d_scores, NT)
                d_values = d_values + dot(dw_ref[0, head:, cols], expo.astype(BF16), NT)
            target[:head, :] = d_keys.astype(BF16)
            target[head:, :] = d_values.astype(BF16)

        @pl.when(count <= 0)
        def _(target=target):
            target[...] = jnp.zeros(target.shape, BF16)


def attend_back(table, base, queries, scaled, d_weighted, sends, keeps, d_query, part=256):
    batch, deep, columns = queries.shape
    head, pair = deep // 4, deep // 2
    chunks = sends + keeps
    size = chunks[0].shape[1]
    each = lambda *shape: pl.BlockSpec((1,) + shape, lambda b: (b, 0, 0))
    stack = pl.BlockSpec((len(sends), 1, pair, size), lambda b: (0, b, 0, 0))
    stacked = [jax.ShapeDtypeStruct((len(sends), batch, pair, size), BF16)] if sends else []
    outs = pl.pallas_call(
        functools.partial(
            attend_back_kernel,
            base=base,
            sends=len(sends),
            keeps=len(keeps),
            first=d_query is None,
            part=part,
        ),
        grid=(batch,),
        in_specs=[
            scalars(),
            each(deep, columns),
            each(head, columns),
            each(pair, columns),
        ]
        + [each(size, pair)] * len(chunks)
        + ([] if d_query is None else [each(head, columns)]),
        out_specs=[each(head, columns)] + [stack] * len(stacked) + [each(pair, size)] * len(keeps),
        out_shape=[jax.ShapeDtypeStruct((batch, head, columns), F32)]
        + stacked
        + [jax.ShapeDtypeStruct((batch, pair, size), BF16)] * len(keeps),
        compiler_params=params(),
        cost_estimate=cost(8, 2),
        name="attend_back",
    )(
        table,
        queries,
        scaled,
        d_weighted,
        *chunks,
        *([] if d_query is None else [d_query]),
    )
    return outs[0], outs[1] if sends else None, outs[len(outs) - len(keeps) :]


def middle_kernel(
    len_ref,
    tok_ref,
    cot_ref,
    exp_ref,
    att_ref,
    gat_ref,
    sum_ref,
    gain_ref,
    wo_in_ref,
    up_ref,
    down_ref,
    out_ref,
    dmid_ref,
    dw_ref,
    dlog_ref,
    keep_ref,
    send_ref,
    gout_ref,
    ggain_ref,
    act_ref,
    din_ref,
    hid_ref,
    dres_ref,
    low_ref,
    spread_ref,
    wo_ref,
    *,
    batch,
    experts,
    chunk,
):
    step = pl.program_id(0)
    _, shard, width = tok_ref.shape
    hidden_units = up_ref.shape[1]
    choices = exp_ref.shape[1]

    @pl.when(step == 0)
    def _():
        wo_ref[...] = wo_in_ref[...].astype(BF16)

    @pl.when(step < batch)
    def _():
        rows = pl.ds(pl.multiple_of(step * shard, shard), shard)
        length = len_ref[step]
        offset = len_ref[batch]
        chosen = exp_ref[0]
        each = [slice(j * shard, (j + 1) * shard) for j in range(choices)]
        which = [chosen[j : j + 1, :] for j in range(choices)]
        gating = [gat_ref[0, :, cols] for cols in each]
        attended = [att_ref[0, :, cols] for cols in each]
        spread = place_experts(which, [g * a for g, a in zip(gating, attended)], experts).astype(BF16)
        spread_ref[:, rows] = spread
        middle = tok_ref[0].astype(F32) + dot(spread, wo_ref[...], TN)
        normed, inv_std = normalize(middle)
        gain = gain_ref[1:2, :]
        hidden = (normed * gain).astype(BF16)
        hid_ref[rows, :] = hidden
        position = offset + lax.broadcasted_iota(jnp.int32, (shard, width), 0)
        d_result = jnp.where(position < length, cot_ref[0].astype(F32), 0.0)
        d_result_low = d_result.astype(BF16)
        dres_ref[rows, :] = d_result_low
        result = middle
        d_hidden = jnp.zeros((shard, width), F32)
        for c in range(hidden_units // chunk):
            cols = slice(c * chunk, (c + 1) * chunk)
            inner = dot(hidden, up_ref[:, cols])
            square = inner * inner
            half = 0.5 * jnp.tanh(inner * (GELU_A + (GELU_A * GELU_B) * square)) + 0.5
            activated = (inner * half).astype(BF16)
            slope = half + (2.0 * inner) * (half - half * half) * (
                GELU_A + (3.0 * GELU_A * GELU_B) * square
            )
            act_ref[rows, cols] = activated
            result = result + dot(activated, down_ref[cols, :])
            d_inner = (dot(d_result_low, down_ref[cols, :], NT) * slope).astype(BF16)
            din_ref[rows, cols] = d_inner
            d_hidden = d_hidden + dot(d_inner, up_ref[:, cols], NT)
        out_ref[0] = result.astype(BF16)
        own_gain = jnp.sum(normed * d_hidden, axis=0, keepdims=True)

        @pl.when(step == 0)
        def _():
            ggain_ref[...] = own_gain

        @pl.when(step > 0)
        def _():
            ggain_ref[...] += own_gain

        d_middle = d_result + norm_back(normed, inv_std, d_hidden * gain)
        dmid_ref[0] = d_middle
        d_middle_low = d_middle.astype(BF16)
        low_ref[rows, :] = d_middle_low
        d_spread = dot(wo_ref[...], d_middle_low, NT)
        d_gating = []
        for j in range(choices):
            selected = pick_expert(which[j], d_spread, experts)
            d_gating.append(jnp.sum(selected * attended[j], axis=0, keepdims=True))
            share = 1.0 / sum_ref[0, :, each[j]]
            d_weighted = selected * (gating[j] * share)
            d_total = split_rows(-(gating[j] * d_gating[j]) * share, d_weighted.shape[0])
            dw_ref[0, :, each[j]] = jnp.concatenate([d_total, d_weighted], axis=0).astype(BF16)
        mixed = functools.reduce(jnp.add, [g * d for g, d in zip(gating, d_gating)])
        expert_row = lax.broadcasted_iota(jnp.int32, (experts, shard), 0)
        d_logits = jnp.zeros((experts, shard), F32)
        for j in range(choices):
            d_logits = d_logits + jnp.where(expert_row == which[j], gating[j] * (d_gating[j] - mixed), 0.0)
        dlog_ref[0] = d_logits.astype(BF16)

    @pl.when(step >= batch)
    def _():
        late = keep_ref.shape[1]
        cols = pl.ds(pl.multiple_of((step - batch) * late, late), late)
        grad_up = dot(hid_ref[...], din_ref[:, cols], TN)
        grad_down = dot(dres_ref[...], act_ref[:, cols], TN)
        first = len_ref[batch + 1] == 0
        keep_ref[...] = jnp.where(first, grad_up, grad_down).astype(BF16)
        send_ref[...] = jnp.where(first, grad_down, grad_up).astype(BF16)

    @pl.when(step == batch)
    def _():
        gout_ref[...] = dot(spread_ref[...], low_ref[...]).astype(BF16)


def middle(limits, tokens, cotangent, chosen, attended, gating, row_sum, gains, wo, up, down, experts):
    batch, shard, width = tokens.shape
    _, head, columns = attended.shape
    choices = chosen.shape[1]
    hidden_units = up.shape[1]
    chunk = 512
    parts = hidden_units // chunk
    full = lambda *shape: pl.BlockSpec(shape, lambda i: (0,) * len(shape))
    each = lambda *shape: pl.BlockSpec((1,) + shape, lambda i: (jnp.minimum(i, batch - 1), 0, 0))
    once = lambda *shape: pl.BlockSpec(
        shape, lambda i: (0,) * len(shape), pipeline_mode=pl.Buffered(1)
    )
    late = lambda i: jnp.maximum(i - batch, 0)
    spread_rows = wo.shape[0]
    total = batch * shard
    return pl.pallas_call(
        functools.partial(middle_kernel, batch=batch, experts=experts, chunk=chunk),
        grid=(batch + parts,),
        in_specs=[
            scalars(),
            each(shard, width),
            each(shard, width),
            each(choices, shard),
            each(head, columns),
            each(1, columns),
            each(1, columns),
            full(*gains.shape),
            once(*wo.shape),
            once(*up.shape),
            once(*down.shape),
        ],
        out_specs=[
            each(shard, width),
            each(shard, width),
            each(2 * head, columns),
            each(experts, shard),
            pl.BlockSpec((width, chunk), lambda i: (0, late(i))),
            pl.BlockSpec((width, chunk), lambda i: (0, late(i))),
            full(*wo.shape),
            full(1, width),
        ],
        out_shape=[
            jax.ShapeDtypeStruct((batch, shard, width), BF16),
            jax.ShapeDtypeStruct((batch, shard, width), F32),
            jax.ShapeDtypeStruct((batch, 2 * head, columns), BF16),
            jax.ShapeDtypeStruct((batch, experts, shard), BF16),
            jax.ShapeDtypeStruct((width, hidden_units), BF16),
            jax.ShapeDtypeStruct((width, hidden_units), BF16),
            jax.ShapeDtypeStruct(wo.shape, BF16),
            jax.ShapeDtypeStruct((1, width), F32),
        ],
        scratch_shapes=[
            pltpu.VMEM((total, hidden_units), BF16),
            pltpu.VMEM((total, hidden_units), BF16),
            pltpu.VMEM((total, width), BF16),
            pltpu.VMEM((total, width), BF16),
            pltpu.VMEM((total, width), BF16),
            pltpu.VMEM((spread_rows, total), BF16),
            pltpu.VMEM(wo.shape, BF16),
        ],
        compiler_params=params(),
        cost_estimate=cost(28, 20),
        name="middle",
    )(limits, tokens, cotangent, chosen, attended, gating, row_sum, gains, wo, up, down)


def query_grad_kernel(hid_ref, dq_ref, exp_ref, dlog_ref, wq_ref, wr_ref, gq_ref, gr_ref, dhid_ref, sum_ref):
    experts = wr_ref.shape[0]
    shard = hid_ref.shape[1]
    head = dq_ref.shape[1]
    choices = exp_ref.shape[1]
    step = pl.program_id(0)
    hidden = hid_ref[0]
    chosen = exp_ref[0]
    which = [chosen[j : j + 1, :] for j in range(choices)]
    blocks = [dq_ref[0, :, j * shard : (j + 1) * shard] * head**-0.5 for j in range(choices)]
    d_query_all = place_experts(which, blocks, experts).astype(BF16)
    d_logits = dlog_ref[0]
    own_query = dot(d_query_all, hidden)
    own_router = dot(d_logits, hidden)

    @pl.when(step == 0)
    def _():
        sum_ref[...] = own_query
        gr_ref[...] = own_router

    @pl.when(step > 0)
    def _():
        sum_ref[...] += own_query
        gr_ref[...] += own_router

    gq_ref[...] = sum_ref[...].astype(BF16)

    dhid_ref[0] = dot(d_query_all, wq_ref[...].astype(BF16), TN) + dot(
        d_logits, wr_ref[...].astype(BF16), TN
    )


def query_grad(hidden, d_query, chosen, d_logits, wq, wr):
    batch, shard, width = hidden.shape
    _, head, columns = d_query.shape
    choices = chosen.shape[1]
    experts = wr.shape[0]
    full = lambda *shape: pl.BlockSpec(shape, lambda b: (0,) * len(shape))
    each = lambda *shape: pl.BlockSpec((1,) + shape, lambda b: (b, 0, 0))
    return pl.pallas_call(
        query_grad_kernel,
        grid=(batch,),
        in_specs=[
            each(shard, width),
            each(head, columns),
            each(choices, shard),
            each(experts, shard),
            full(*wq.shape),
            full(*wr.shape),
        ],
        out_specs=[full(*wq.shape), full(*wr.shape), each(shard, width)],
        out_shape=[
            jax.ShapeDtypeStruct(wq.shape, BF16),
            jax.ShapeDtypeStruct(wr.shape, F32),
            jax.ShapeDtypeStruct((batch, shard, width), F32),
        ],
        scratch_shapes=[pltpu.VMEM(wq.shape, F32)],
        compiler_params=params(),
        cost_estimate=cost(2, 6),
        name="query_grad",
    )(hidden, d_query, chosen, d_logits, wq, wr)


def input_grad_kernel(
    tok_ref,
    hid_ref,
    dpair_ref,
    dhid_ref,
    dmid_ref,
    gain_ref,
    wkv_ref,
    query_ref,
    out_ref,
    router_ref,
    two_ref,
    gin_ref,
    tail_ref,
    gkv_ref,
    one_ref,
):
    step = pl.program_id(0)
    normed, inv_std = normalize(tok_ref[0].astype(F32))
    d_pair = dpair_ref[0]
    d_hidden = dhid_ref[0] + dot(d_pair, wkv_ref[...].astype(BF16), TN)
    own_pair = dot(d_pair, hid_ref[0])
    own_gain = jnp.sum(normed * d_hidden, axis=0, keepdims=True)

    @pl.when(step == 0)
    def _():
        gkv_ref[...] = own_pair
        one_ref[...] = own_gain

    @pl.when(step > 0)
    def _():
        gkv_ref[...] += own_pair
        one_ref[...] += own_gain

    d_inputs = dmid_ref[0] + norm_back(normed, inv_std, d_hidden * gain_ref[0:1, :])
    gin_ref[0] = d_inputs.astype(BF16)
    query_rows, width = query_ref.shape
    head_rows = query_rows + out_ref.shape[0]
    used = head_rows + gkv_ref.shape[0] + router_ref.shape[0] + 2
    blank = jnp.zeros((tail_ref.shape[0] - used, width), F32)
    small = [gkv_ref[...], router_ref[...], one_ref[...], two_ref[...], blank]
    tail_ref[:query_rows, :] = query_ref[...]
    tail_ref[query_rows:head_rows, :] = out_ref[...]
    tail_ref[head_rows:, :] = jnp.concatenate(small, axis=0).astype(BF16)


def input_grad(
    tokens, hidden, d_pair, d_hidden, d_middle, gains, wkv, grad_query, grad_out, grad_router, grad_gain_two
):
    batch, shard, width = tokens.shape
    pair = wkv.shape[0]
    rows = -(-(grad_query.shape[0] + grad_out.shape[0] + pair + grad_router.shape[0] + 2) // 64) * 64
    full = lambda *shape: pl.BlockSpec(shape, lambda b: (0,) * len(shape))
    each = lambda *shape: pl.BlockSpec((1,) + shape, lambda b: (b, 0, 0))
    return pl.pallas_call(
        input_grad_kernel,
        grid=(batch,),
        in_specs=[
            each(shard, width),
            each(shard, width),
            each(pair, shard),
            each(shard, width),
            each(shard, width),
            full(*gains.shape),
            full(*wkv.shape),
            full(*grad_query.shape),
            full(*grad_out.shape),
            full(*grad_router.shape),
            full(*grad_gain_two.shape),
        ],
        out_specs=[each(shard, width), full(rows, width)],
        out_shape=[
            jax.ShapeDtypeStruct((batch, shard, width), BF16),
            jax.ShapeDtypeStruct((rows, width), BF16),
        ],
        scratch_shapes=[pltpu.VMEM(wkv.shape, F32), pltpu.VMEM((1, width), F32)],
        compiler_params=params(),
        cost_estimate=cost(2, 9),
        name="input_grad",
    )(tokens, hidden, d_pair, d_hidden, d_middle, gains, wkv, grad_query, grad_out, grad_router, grad_gain_two)


def square_fine(matrix):
    high = matrix.astype(BF16)
    rest = (matrix - high.astype(F32)).astype(BF16)
    cross = dot(high, rest)
    return dot(high, high) + (cross + cross.T)


def mirrored(left, bottom):
    half = bottom.shape[0]
    right = jnp.concatenate([left[half:].T, bottom], axis=0)
    return jnp.concatenate([left, right], axis=1)


def gram_of(low):
    half = low.shape[0] // 2
    return mirrored(dot(low, low[:half], NT), dot(low[half:], low[half:], NT))


def square_of(gram):
    half = gram.shape[0] // 2
    high = gram.astype(BF16)
    rest = (gram - high.astype(F32)).astype(BF16)
    cross = dot(high, rest)
    return mirrored(dot(high, high[:, :half]), dot(high[half:], high[:, half:])) + (cross + cross.T)


def muon_kernel(core_ref, up_ref, down_ref, grad_in_ref, solved_ref, x_ref, low_ref, turn_ref, grad_ref, sems):
    rows, cols = x_ref.shape
    fetch = pltpu.make_async_copy(grad_in_ref, grad_ref, sems.at[0])
    fetch.start()

    @pl.when(core_ref[0] == 0)
    def _():
        copy = pltpu.make_async_copy(up_ref, x_ref, sems.at[1])
        copy.start()
        copy.wait()

    @pl.when(core_ref[0] != 0)
    def _():
        pieces = range(0, cols, rows)
        copies = [
            pltpu.make_async_copy(
                down_ref.at[pl.ds(at, rows), :], turn_ref.at[pl.ds(at, rows), :], sems.at[2 + index]
            )
            for index, at in enumerate(pieces)
        ]
        for copy in copies:
            copy.start()
        for copy, at in zip(copies, pieces):
            copy.wait()
            x_ref[:, at : at + rows] = turn_ref[at : at + rows, :].T

    fetch.wait()

    renewed = MOMENT_DECAY * x_ref[...] + grad_ref[:, :cols].astype(F32)
    inverse = 1.0 / (jnp.sqrt(jnp.sum(renewed * renewed)) + 1e-07)
    first = renewed * inverse
    x_ref[...] = first
    low_ref[...] = first.astype(BF16)

    def iterate(_, carry):
        low = low_ref[...]
        gram = gram_of(low)
        poly = (NEWTON_B * gram + NEWTON_C * square_of(gram)).astype(BF16)
        following = NEWTON_A * x_ref[...] + dot(poly, low)
        x_ref[...] = following
        low_ref[...] = following.astype(BF16)
        return carry

    lax.fori_loop(0, 5, iterate, 0)
    solved_ref[...] = low_ref[...]


def muon(core_ref, up_mom, down_mom, grad):
    anywhere = pl.BlockSpec(memory_space=pl.ANY)
    return pl.pallas_call(
        muon_kernel,
        in_specs=[scalars(), anywhere, anywhere, anywhere],
        out_specs=whole(),
        out_shape=jax.ShapeDtypeStruct(up_mom.shape, BF16),
        scratch_shapes=[
            pltpu.VMEM(up_mom.shape, F32),
            pltpu.VMEM(up_mom.shape, BF16),
            pltpu.VMEM(down_mom.shape, F32),
            pltpu.VMEM(grad.shape, BF16),
            pltpu.SemaphoreType.DMA((2 + max(down_mom.shape) // min(down_mom.shape),)),
        ],
        compiler_params=params(),
        cost_estimate=cost(25, 8),
        name="muon",
    )(core_ref, up_mom, down_mom, grad)


def prepare_kernel(up_ref, down_ref, up_low_ref, down_low_ref, up_square_ref, down_square_ref):
    for ref, low_ref, square_ref in (
        (up_ref, up_low_ref, up_square_ref),
        (down_ref, down_low_ref, down_square_ref),
    ):
        weight = ref[...]
        low_ref[...] = weight.astype(BF16)
        total = jnp.sum(jnp.sum(weight * weight, axis=0, keepdims=True), axis=1, keepdims=True)

        @pl.when(pl.program_id(0) == 0)
        def _(square_ref=square_ref, total=total):
            square_ref[...] = total

        @pl.when(pl.program_id(0) > 0)
        def _(square_ref=square_ref, total=total):
            square_ref[...] += total


def prepare(up, down, steps=4):
    rows, cols = up.shape
    one = pl.BlockSpec((1, 1), lambda i: (0, 0))
    flat = pl.BlockSpec((rows // steps, cols), lambda i: (i, 0))
    turned = pl.BlockSpec((cols // steps, rows), lambda i: (i, 0))
    return pl.pallas_call(
        prepare_kernel,
        grid=(steps,),
        in_specs=[flat, turned],
        out_specs=[flat, turned, one, one],
        out_shape=[
            jax.ShapeDtypeStruct(up.shape, BF16),
            jax.ShapeDtypeStruct(down.shape, BF16),
            jax.ShapeDtypeStruct((1, 1), F32),
            jax.ShapeDtypeStruct((1, 1), F32),
        ],
        compiler_params=params(),
        cost_estimate=cost(1, 12),
        name="prepare",
    )(up, down)


def blend_block(first, square_refs, refs, rank):
    up_ref, down_ref, own_rows, other_rows, own_cols, other_cols, up_out, down_out = refs
    for ref, out, one, two, turn in (
        (up_ref, up_out, own_rows, other_rows, False),
        (down_ref, down_out, other_cols, own_cols, True),
    ):
        change = jnp.where(first, one[...].astype(F32), two[...].astype(F32))
        change = change.T if turn else change
        if square_refs:
            step = jnp.sqrt(square_refs[1 if turn else 0][...]) * (STEP_RATE / math.sqrt(rank))
            out[...] = ref[...] - step * change
        else:
            out[...] = MOMENT_DECAY * ref[...] + change


def blend_specs(up, down, steps):
    rows, cols = up.shape
    flat = pl.BlockSpec((rows // steps, cols), lambda i, core: (i, 0))
    turned = pl.BlockSpec((cols // steps, rows), lambda i, core: (i, 0))

    def wanted(i, core, turn):
        return jnp.where(core[0] == turn, i, 0)

    row_specs = [
        pl.BlockSpec((rows // steps, cols), lambda i, core, turn=turn: (wanted(i, core, turn), 0)) for turn in (0, 1)
    ]
    col_specs = [
        pl.BlockSpec((rows, cols // steps), lambda i, core, turn=turn: (0, wanted(i, core, turn))) for turn in (1, 0)
    ]
    return [flat, turned] + row_specs + col_specs, [flat, turned]


def by_block(values, sizes, finish):
    pieces = []
    at = 0
    for size in sizes:
        piece = values[at : at + size]
        total = jnp.sum(jnp.sum(piece * piece, axis=1, keepdims=True), axis=0, keepdims=True)
        pieces.append(jnp.broadcast_to(finish(total, size), (size, 1)))
        at += size
    return jnp.concatenate(pieces, axis=0)


def block_ids(sizes, axis):
    index = lax.broadcasted_iota(jnp.int32, (sum(sizes), sum(sizes)), axis)
    ids = jnp.zeros(index.shape, jnp.int32)
    at = 0
    for size in sizes[:-1]:
        at += size
        ids = ids + (index >= at).astype(jnp.int32)
    return ids


def solve_packs(step, sizes, x_ref, renew, weights_of, store):
    @pl.when(step == 0)
    def _():
        for index, moment in enumerate(renew()):
            x_ref[index] = moment * by_block(moment, sizes, lambda total, _: 1.0 / (jnp.sqrt(total) + 1e-07))

    @pl.when((step >= 1) & (step <= 5))
    def _():
        same = block_ids(sizes, 0) == block_ids(sizes, 1)
        matrices = [x_ref[index] for index in range(x_ref.shape[0])]
        lows = [matrix.astype(BF16) for matrix in matrices]
        grams = [jnp.where(same, dot(low, low, NT), 0.0) for low in lows]
        squares = [square_fine(gram) for gram in grams]
        polys = [(NEWTON_B * g + NEWTON_C * q).astype(BF16) for g, q in zip(grams, squares)]
        for index, (matrix, poly, low) in enumerate(zip(matrices, polys, lows)):
            x_ref[index] = NEWTON_A * matrix + dot(poly, low)

    @pl.when(step == 6)
    def _():
        fresh = []
        for index, (weight, ranks) in enumerate(weights_of()):
            factors = iter([STEP_RATE / math.sqrt(min(weight.shape[1], rank)) for rank in ranks])
            scale = by_block(weight, sizes, lambda total, _: jnp.sqrt(total) * next(factors))
            fresh.append(weight - scale * x_ref[index])
        store(fresh)


STEPS = 8


def renew_kernel(core_ref, *refs):
    blend_block(core_ref[0] == 0, [], refs, min(refs[2].shape))


def renew(core_ref, up_mom, down_mom, own, other):
    ins, outs = blend_specs(up_mom, down_mom, STEPS)
    return pl.pallas_call(
        renew_kernel,
        grid_spec=pltpu.PrefetchScalarGridSpec(num_scalar_prefetch=1, grid=(STEPS,), in_specs=ins, out_specs=outs),
        out_shape=[jax.ShapeDtypeStruct(array.shape, F32) for array in (up_mom, down_mom)],
        compiler_params=params(),
        cost_estimate=cost(1, 20),
        name="renew",
    )(core_ref, up_mom, down_mom, own, other, own, other)


def move_kernel(core_ref, *refs, head, gain_rate, rank):
    square_refs = refs[:2]
    blend_refs = refs[2:8] + refs[19:21]
    wq_ref, wo_ref, wkv_ref, wr_ref, gain_ref, mq_ref, mo_ref, mkv_ref, mr_ref, mgain_ref, tail_ref = refs[8:19]
    wq_out, wo_out, wkv_out, wr_out, gain_out, mq_out, mo_out, mkv_out, mr_out, mgain_out, x_ref = refs[21:]
    sizes = (head,) * 4
    rows = sum(sizes)
    query_rows, pair, experts = wq_ref.shape[0], wkv_ref.shape[0], wr_ref.shape[0]
    head_rows = query_rows + wo_ref.shape[0]
    places = [
        (weight, moment, target, slice(at, at + rows))
        for weight, moment, target in ((wq_ref, mq_out, wq_out), (wo_ref, mo_out, wo_out))
        for at in range(0, weight.shape[0], rows)
    ]
    blank = jnp.zeros((rows - pair - experts, wkv_ref.shape[1]), F32)

    def renewed():
        mq_out[...] = MOMENT_DECAY * mq_ref[...] + tail_ref[:query_rows, :].astype(F32)
        mo_out[...] = MOMENT_DECAY * mo_ref[...] + tail_ref[query_rows:head_rows, :].astype(F32)
        small = tail_ref[head_rows:, :].astype(F32)
        mkv_out[...] = MOMENT_DECAY * mkv_ref[...] + small[:pair]
        mr_out[...] = MOMENT_DECAY * mr_ref[...] + small[pair : pair + experts]
        gain_moment = MOMENT_DECAY * mgain_ref[...] + small[pair + experts : pair + experts + 2]
        mgain_out[...] = gain_moment
        gain_out[...] = gain_ref[...] - gain_rate * gain_moment
        last = jnp.concatenate([mkv_out[...], mr_out[...], blank], axis=0)
        return [moment[at, :] for _, moment, _, at in places] + [last]

    def weights_of():
        last = jnp.concatenate([wkv_ref[...], wr_ref[...], blank], axis=0)
        return [(weight[at, :], sizes) for weight, _, _, at in places] + [(last, (head, head, experts, head))]

    def store(fresh):
        for (_, _, target, at), value in zip(places, fresh):
            target[at, :] = value
        wkv_out[...] = fresh[-1][:pair]
        wr_out[...] = fresh[-1][pair : pair + experts]

    solve_packs(pl.program_id(0), sizes, x_ref, renewed, weights_of, store)
    blend_block(core_ref[0] == 0, square_refs, blend_refs, rank)


def move_and_tail(core_ref, squares, up, down, own, other, weights, moments, tail, head, gain_rate):
    ins, outs = blend_specs(up, down, STEPS)
    one = pl.BlockSpec((1, 1), lambda i, core: (0, 0))
    full = lambda array: pl.BlockSpec(array.shape, lambda i, core: (0, 0))
    arrays = weights + moments
    rows = 4 * head
    return pl.pallas_call(
        functools.partial(move_kernel, head=head, gain_rate=gain_rate, rank=min(up.shape)),
        grid_spec=pltpu.PrefetchScalarGridSpec(
            num_scalar_prefetch=1,
            grid=(STEPS,),
            in_specs=[one, one] + ins + [full(array) for array in arrays + [tail]],
            out_specs=outs + [full(array) for array in arrays],
            scratch_shapes=[pltpu.VMEM(((weights[0].shape[0] + weights[1].shape[0]) // rows + 1, rows, up.shape[0]), F32)],
        ),
        out_shape=[jax.ShapeDtypeStruct(array.shape, F32) for array in [up, down] + arrays],
        compiler_params=params(),
        cost_estimate=cost(1, 20),
        name="move_and_tail",
    )(core_ref, *squares, up, down, own, other, own, other, *arrays, tail)


def after(*values):
    return lax.optimization_barrier(values)


class Sums:
    def __init__(self):
        self.planes, self.lines = lax.axis_size("dp"), lax.axis_size("seq")
        plane_bits = range(self.planes.bit_length() - 1)
        self.orders = [[(1 << bit, 0) for bit in bits] for bits in (plane_bits, reversed(plane_bits))]
        self.plane, self.line = lax.axis_index("dp"), lax.axis_index("seq")
        self.table = None

    def send(self, value, pairs):
        if self.table is not None:
            value, self.table = after(value, self.table)
        return lax.ppermute(value, ("dp", "seq"), pairs)

    def exchange(self, value, flips):
        pairs = []
        for plane in range(self.planes):
            for line in range(self.lines):
                flip = flips[line % 2]
                pairs.append((plane * self.lines + line, (plane ^ flip[0]) * self.lines + (line ^ flip[1])))
        return self.send(value, pairs)

    def stages(self):
        return list(zip(*self.orders))

    def upper(self, flips):
        sides = [((self.plane & flip[0]) | (self.line & flip[1])) != 0 for flip in flips]
        return jnp.where(self.line % 2 == 0, sides[0], sides[1])

    def sibling(self, value):
        return self.exchange(value, ((0, 1), (0, 1)))

    def add_up(self, *terms):
        return functools.reduce(jnp.add, [term.astype(F32) for term in terms]).astype(terms[0].dtype)

    def halve(self, rows, upper, flips):
        half = rows.shape[0] // 2
        low, high = rows[:half], rows[half:]
        return self.exchange(jnp.where(upper, low, high), flips), jnp.where(upper, high, low)

    def join(self, rows, arrived, upper):
        return jnp.concatenate([jnp.where(upper, arrived, rows), jnp.where(upper, rows, arrived)], axis=0)

    def to_chip(self, value, mask):
        return self.exchange(value, ((0, 2 * mask), (0, 2 * mask)))


def per_device(
    tokens_in,
    cotangent,
    lengths,
    experts_top,
    gains,
    router,
    query_w,
    key_value_w,
    out_w,
    up_w,
    down_w,
    gains_mom,
    router_mom,
    query_mom,
    key_value_mom,
    out_mom,
    up_mom,
    down_mom,
):
    batch_here, shard_len, width = tokens_in.shape
    experts, _, head = query_w.shape
    seq_devices = lax.axis_size("seq")
    seq_len = shard_len * seq_devices
    token_total = batch_here * lax.axis_size("dp") * seq_len

    def wide(stacked):
        return jnp.swapaxes(stacked, -1, -2).reshape(-1, width)

    def narrow(rows):
        return jnp.swapaxes(rows.reshape(-1, head, width), -1, -2)

    chosen = jnp.swapaxes(experts_top, 1, 2)
    wq, wkv, wr = wide(query_w), wide(key_value_w), router.T
    wo = out_w.reshape(-1, width)
    sums = Sums()
    place = lax.axis_index("seq").astype(jnp.int32)
    core, chip = place % 2, place // 2
    chips = seq_devices // 2
    core_ref = core[None]

    rounds = [
        [away for away in range(chips) if away.bit_count() == bits] for bits in range(chips.bit_length())
    ]
    own_turns = [[(away, core) for away in members] for members in rounds]
    sibling_turns = [[(away, 1 - core) for away in members] for members in rounds]
    forward = [own_turns[0] + sibling_turns[0]] + own_turns[1:] + [[]]
    for turn in range(1, len(rounds)):
        forward[turn + 1] = sibling_turns[turn] + forward[turn + 1]
    last = len(rounds)
    sends_of = [rounds[last - 1 - call] for call in range(last)] + [[]]
    sends_of[last - 2], sends_of[last - 1] = sends_of[last - 2] + rounds[0], []
    keeps_of = [[]] + rounds[::-1]
    backward = [
        [(away, 1 - core) for away in theirs] + [(away, core) for away in ours]
        for theirs, ours in zip(sends_of, keeps_of)
    ]
    bases, starts = [], []
    for group in forward + backward:
        bases.append(batch_here + 2 + len(starts))
        starts += [(2 * (chip ^ away) + which) * shard_len for away, which in group]
    table = jnp.concatenate([lengths, jnp.stack([place * shard_len, core] + starts)])

    hidden, key_value, queries, scaled, gating = project(tokens_in, chosen, gains, wq, wkv, wr)
    sums.table = table
    blocks, siblings = {0: key_value}, {0: sums.sibling(key_value)}
    incoming = [sums.to_chip(key_value, away) for away in rounds[1]]
    state = attend(sums.table, bases[0], queries, [blocks[0], siblings[0]], None, False)
    up_late, state = after(up_w, state)
    up_low, down_low, *squares = prepare(up_late, down_w)
    squares, sums.table = after(squares, sums.table)
    for turn in range(1, len(rounds) + 1):
        group = []
        if turn > 1:
            group += [siblings[away] for away in rounds[turn - 1]]
        if turn < len(rounds):
            incoming, state, sums.table = after(incoming, state, sums.table)
            blocks.update(zip(rounds[turn], incoming))
            group += incoming
            incoming = [
                sums.to_chip(blocks[away & (away - 1)], away & -away)
                for away in (rounds[turn + 1] if turn + 1 < len(rounds) else [])
            ]
            siblings.update((away, sums.sibling(blocks[away])) for away in rounds[turn])
        state = attend(sums.table, bases[turn], queries, group, state, turn == len(rounds))
    attended, row_sum, back_queries = state
    (
        layer_out,
        d_middle,
        d_weighted,
        d_logits,
        keep,
        send,
        grad_out,
        grad_gain_two,
    ) = middle(
        sums.table,
        tokens_in,
        cotangent,
        chosen,
        attended,
        gating,
        row_sum,
        gains,
        wo,
        up_low,
        down_low,
        experts,
    )
    stages = sums.stages()

    def halving(flips):
        def step(arrived):
            return list(sums.halve(sums.add_up(*arrived), sums.upper(flips), flips))

        return step

    def doubling(flips):
        def step(arrived):
            return [arrived[0], sums.exchange(arrived[0], flips)]

        return step

    def joined(flips, step):
        return lambda arrived: step([sums.join(*arrived, sums.upper(flips))])

    stages += [((0, 2 << bit), (0, 2 << bit)) for bit in range(chips.bit_length() - 1)]
    back = stages[::-1]
    ffn_steps = [halving(flips) for flips in stages]
    ffn_steps.append(lambda arrived: doubling(back[0])([sums.add_up(*arrived)]))
    for earlier, flips in zip(back, back[1:]):
        ffn_steps.append(joined(earlier, doubling(flips)))

    ffn = [sums.sibling(send), keep]
    d_query, crossing, arrived = None, {}, {}
    grown = {away: [] for away in range(chips)}
    for call in range(last + 1):
        theirs, ours = sends_of[call], keeps_of[call]
        d_query, d_send, d_keeps = attend_back(
            sums.table,
            bases[last + 1 + call],
            back_queries,
            scaled,
            d_weighted,
            [siblings[away] for away in theirs],
            [blocks[away] for away in ours],
            d_query,
        )
        if call == last:
            break
        d_query, d_send, ffn, crossing, grown = after(d_query, d_send, ffn, crossing, grown)
        if len(ffn_steps) > 5:
            ffn = ffn_steps.pop(0)(ffn)
        arrived.update(crossing)
        crossing = {}
        if theirs:
            exchanged = sums.sibling(d_send)
            crossing = {away: exchanged[i] for i, away in enumerate(theirs)}
        for away, d_keep in zip(ours, d_keeps):
            total = sums.add_up(d_keep, arrived[away], *grown[away])
            grown[away ^ (away & -away)].append(sums.to_chip(total, away & -away))

    sums.table = core_ref
    ffn, d_query = after(ffn, d_query)
    while len(ffn_steps) > 4:
        ffn = ffn_steps.pop(0)(ffn)
    hidden, sums.table = after(hidden, sums.table)
    grad_query, grad_router, d_hidden = query_grad(hidden, d_query, chosen, d_logits, wq, wr)
    sides = [d_keeps[0], arrived[0], *grown[0]]
    ffn, sides, grad_query = after(ffn, sides, grad_query)
    ffn = ffn_steps.pop(0)(ffn)
    d_hidden, sides, sums.table = after(d_hidden, sides, sums.table)
    input_gradient, tail = input_grad(
        tokens_in,
        hidden,
        sums.add_up(*sides),
        d_hidden,
        d_middle,
        gains,
        wkv,
        grad_query,
        grad_out,
        grad_router,
        grad_gain_two,
    )
    second = core == 1
    ffn, tail = after(ffn, tail)
    ffn = ffn_steps.pop(0)(ffn)
    plane_stages = sums.stages()
    plane_back = plane_stages[::-1]
    tail_steps = [halving(flips) for flips in plane_stages]
    tail_steps += [lambda arrived, flips=flips: doubling(flips)([sums.add_up(*arrived)]) for flips in back[::-1][len(plane_back) :]]
    tail_steps.append(lambda arrived: doubling(plane_back[0])([sums.add_up(*arrived)]))
    tail_steps += [joined(earlier, doubling(flips)) for earlier, flips in zip(plane_back, plane_back[1:])]

    def tail_step(tail):
        tail, sums.table = after(tail, sums.table)
        return tail_steps.pop(0)(tail)

    tail = list(sums.halve(tail, second, ((0, 1), (0, 1))))
    tail = tail_step(tail)
    ffn, sums.table = after(ffn, sums.table)
    ffn = ffn_steps.pop(0)(ffn)
    tail = tail_step(tail)
    ffn, sums.table = after(ffn, sums.table)
    ffn = ffn_steps.pop(0)(ffn)
    while len(tail_steps) > 1:
        tail = tail_step(tail)
    ffn, sums.table = after(ffn, sums.table)
    own_ffn = sums.join(*ffn, sums.upper(back[-1]))
    other_ffn = sums.sibling(own_ffn)
    solved_ffn = muon(sums.table, up_mom, down_mom, own_ffn)
    tail, other_ffn, solved_ffn = after(tail, other_ffn, solved_ffn)
    other_solved = sums.sibling(solved_ffn)
    tail = tail_step(tail)
    up_mom_new, down_mom_new = renew(sums.table, up_mom, down_mom, own_ffn, other_ffn)
    tail, other_solved, up_mom_new = after(tail, other_solved, up_mom_new)
    tail = sums.join(*tail, sums.upper(plane_back[-1]))
    tail = sums.join(tail, sums.sibling(tail), second)
    (
        up_new,
        down_new,
        query_new,
        out_new,
        pair_new,
        router_new,
        gains_new,
        query_mom_new,
        out_mom_new,
        pair_mom_new,
        router_mom_new,
        gains_mom_new,
    ) = move_and_tail(
        sums.table,
        squares,
        up_w,
        down_w,
        solved_ffn,
        other_solved,
        [wq, wo, wkv, wr, gains],
        [wide(query_mom), out_mom.reshape(-1, width), wide(key_value_mom), router_mom.T, gains_mom],
        tail,
        head,
        GAIN_RATE / math.sqrt(token_total),
    )
    return (
        layer_out,
        input_gradient,
        gains_new,
        gains_mom_new,
        router_new.T,
        router_mom_new.T,
        narrow(query_new),
        narrow(query_mom_new),
        narrow(pair_new),
        narrow(pair_mom_new),
        out_new.reshape(out_w.shape),
        out_mom_new.reshape(out_w.shape),
        up_new,
        up_mom_new,
        down_new,
        down_mom_new,
    )


def solution(mesh):
    split = P("dp", "seq", None)
    return jax.shard_map(
        per_device,
        mesh=mesh,
        in_specs=(split, split, P("dp"), split) + (P(),) * 14,
        out_specs=(split, split) + (P(),) * 14,
        check_vma=False,
    )
```

```python
import functools
import math

import jax
import jax.numpy as jnp
from jax import lax
from jax.experimental import pallas as pl
from jax.experimental.pallas import tpu as pltpu
from jax.sharding import PartitionSpec as P

EPSILON = 1e-05
NEWTON_A = 3.4445
NEWTON_B = -4.775
NEWTON_C = 2.0315
STEP_RATE = 0.3
GAIN_RATE = 0.1
MOMENT_DECAY = 0.5
LOG2E = math.log2(math.e)
GELU_A = math.sqrt(2.0 / math.pi)
GELU_B = 0.044715
MASKED = -1e30
MIB = 1 << 20

F32 = jnp.float32
BF16 = jnp.bfloat16

NN = (((1,), (0,)), ((), ()))
NT = (((1,), (1,)), ((), ()))
TN = (((0,), (0,)), ((), ()))


def dot(left, right, dims=NN):
    return lax.dot_general(left, right, dims, preferred_element_type=F32)


def params(mib=58):
    return pltpu.CompilerParams(vmem_limit_bytes=mib * MIB)


def cost(giga, mib=4, exps=0):
    return pl.CostEstimate(flops=int(giga * 1e7), bytes_accessed=mib * 4096, transcendentals=exps)


def whole():
    return pl.BlockSpec(memory_space=pltpu.VMEM)


def scalars():
    return pl.BlockSpec(memory_space=pltpu.SMEM)


def normalize(values_in):
    average = jnp.mean(values_in, axis=-1, keepdims=True)
    centred = values_in - average
    inv_std = lax.rsqrt(jnp.mean(centred * centred, axis=-1, keepdims=True) + EPSILON)
    return centred * inv_std, inv_std


def norm_back(normed, inv_std, d_normed):
    first = jnp.mean(d_normed, axis=-1, keepdims=True)
    second = jnp.mean(d_normed * normed, axis=-1, keepdims=True)
    return inv_std * (d_normed - first - normed * second)


def split_rows(row, count):
    index = lax.broadcasted_iota(jnp.int32, (count, row.shape[1]), 0)
    block = jnp.zeros((count, row.shape[1]), F32)
    for term in range(3):
        part = row.astype(BF16).astype(F32)
        block = jnp.where(index == term, part, block)
        row = row - part
    return block


def pick_expert(row, stacked, experts):
    size = stacked.shape[0] // experts
    total = jnp.where(row == 0, stacked[:size], 0.0)
    for expert in range(1, experts):
        total = total + jnp.where(row == expert, stacked[expert * size : (expert + 1) * size], 0.0)
    return total


def place_experts(rows, blocks, experts):
    pieces = []
    for expert in range(experts):
        piece = jnp.where(rows[0] == expert, blocks[0], 0.0)
        for row, block in zip(rows[1:], blocks[1:]):
            piece = piece + jnp.where(row == expert, block, 0.0)
        pieces.append(piece)
    return jnp.concatenate(pieces, axis=0)


def project_kernel(
    tok_ref, exp_ref, gain_ref, wq_ref, wkv_ref, wr_ref, hid_ref, kv_ref, q_ref, scaled_ref, gat_ref
):
    experts = wr_ref.shape[0]
    shard = tok_ref.shape[1]
    head = wkv_ref.shape[0] // 2
    ones = (lax.broadcasted_iota(jnp.int32, (2 * head, shard), 0) == 0).astype(F32)
    normed, _ = normalize(tok_ref[0].astype(F32))
    hidden = (normed * gain_ref[0:1, :]).astype(BF16)
    hid_ref[0] = hidden
    kv_ref[0] = dot(hidden, wkv_ref[...].astype(BF16), NT).astype(BF16)
    query_all = dot(wq_ref[...].astype(BF16), hidden, NT)
    logits = dot(wr_ref[...].astype(BF16), hidden, NT)
    chosen = exp_ref[0]
    choices = chosen.shape[0]
    picked = []
    for j in range(choices):
        row = chosen[j : j + 1, :]
        cols = slice(j * shard, (j + 1) * shard)
        query = pick_expert(row, query_all, experts).astype(BF16).astype(F32)
        exponent = query * (head**-0.5 * LOG2E)
        high = exponent.astype(BF16).astype(F32)
        q_ref[0, :, cols] = jnp.concatenate([high, exponent - high, ones], axis=0).astype(BF16)
        scaled_ref[0, :, cols] = (query * head**-0.5).astype(BF16)
        picked.append(pick_expert(row, logits, experts))
    top = functools.reduce(jnp.maximum, picked)
    raised = [jnp.exp(value - top) for value in picked]
    total = functools.reduce(jnp.add, raised)
    for j in range(choices):
        gat_ref[0, :, j * shard : (j + 1) * shard] = raised[j] / total


def project(tokens, chosen, gains, wq, wkv, wr):
    batch, shard, width = tokens.shape
    choices = chosen.shape[1]
    head = wkv.shape[0] // 2
    columns = choices * shard
    full = lambda array: pl.BlockSpec(array.shape, lambda b: (0,) * array.ndim)
    each = lambda *shape: pl.BlockSpec((1,) + shape, lambda b: (b, 0, 0))
    return pl.pallas_call(
        project_kernel,
        grid=(batch,),
        in_specs=[each(shard, width), each(choices, shard), full(gains), full(wq), full(wkv), full(wr)],
        out_specs=[
            each(shard, width),
            each(shard, 2 * head),
            each(4 * head, columns),
            each(head, columns),
            each(1, columns),
        ],
        out_shape=[
            jax.ShapeDtypeStruct((batch, shard, width), BF16),
            jax.ShapeDtypeStruct((batch, shard, 2 * head), BF16),
            jax.ShapeDtypeStruct((batch, 4 * head, columns), BF16),
            jax.ShapeDtypeStruct((batch, head, columns), BF16),
            jax.ShapeDtypeStruct((batch, 1, columns), F32),
        ],
        compiler_params=params(),
        cost_estimate=cost(4, 4),
        name="project",
    )(tokens, chosen, gains, wq, wkv, wr)


def spread_keys(block, count):
    rows, pair = block.shape
    head = pair // 2
    lane = lax.broadcasted_iota(jnp.int32, block.shape, 1)
    position = lax.broadcasted_iota(jnp.int32, block.shape, 0)
    twice = jnp.where(lane < head, block, pltpu.roll(block, head, 1))
    mask = jnp.where(position >= count, MASKED, 0.0)
    extra = jnp.where(lane == 0, mask, jnp.where(lane <= 3, 1.0, 0.0))
    return jnp.concatenate([twice, extra], axis=1).astype(BF16)


def attend_kernel(*refs, base, chunks, first, last, part):
    refs = list(refs)
    tab_ref, q_ref = refs[:2]
    kv_refs = refs[2 : 2 + chunks]
    rest = refs[2 + chunks :]
    if first:
        state = None
    else:
        state, rest = rest[:2], rest[2:]
    max_ref, acc_ref = rest[-2:]
    rest = rest[:-2]
    columns = q_ref.shape[2]
    head = q_ref.shape[1] // 4
    length = tab_ref[pl.program_id(0)]
    if first:
        max_ref[...] = jnp.full(max_ref.shape, MASKED, F32)
        acc_ref[...] = jnp.zeros_like(acc_ref)
    else:
        max_ref[...] = state[0][0]
        acc_ref[...] = state[1][0]
    parts = [slice(at, at + part) for at in range(0, columns, part)]
    for index, kv_ref in enumerate(kv_refs):
        count = length - tab_ref[base + index]

        @pl.when(count > 0)
        def _(kv_ref=kv_ref, count=count):
            block = kv_ref[0].astype(F32)
            keys = spread_keys(block, count)
            extra = acc_ref.shape[0] - head
            values = jnp.concatenate(
                [block.T[head:].astype(BF16), jnp.ones((extra, block.shape[0]), BF16)], axis=0
            )
            before = [max_ref[:, cols] for cols in parts]
            sums = [acc_ref[:, cols] for cols in parts]
            scores = [dot(keys, q_ref[0, :, cols]) for cols in parts]
            after = [
                jnp.maximum(old, jnp.max(score, axis=0, keepdims=True))
                for old, score in zip(before, scores)
            ]
            expos = [jnp.exp2(score - new).astype(BF16) for score, new in zip(scores, after)]
            shrinks = [jnp.exp2(old - new) for old, new in zip(before, after)]
            sums = [total * shrink + dot(values, expo) for total, shrink, expo in zip(sums, shrinks, expos)]
            for cols, new, total in zip(parts, after, sums):
                max_ref[:, cols] = new
                acc_ref[:, cols] = total

    if last:
        att_ref, sum_ref, back_ref = rest
        row_sum = acc_ref[head : head + 1, :]
        sum_ref[0] = row_sum
        att_ref[0] = acc_ref[:head, :] / row_sum
        back_ref[0, : 2 * head, :] = q_ref[0, : 2 * head, :]
        ones = (lax.broadcasted_iota(jnp.int32, (1, columns), 0) == 0).astype(F32)
        tail = jnp.concatenate([ones, split_rows(-max_ref[...], 2 * head - 1)], axis=0)
        back_ref[0, 2 * head :, :] = tail.astype(BF16)
    else:
        rest[0][0] = max_ref[...]
        rest[1][0] = acc_ref[...]


def attend(table, base, queries, chunks, state, last, part=256):
    batch, deep, columns = queries.shape
    head = deep // 4
    tall = head + 16
    each = lambda *shape: pl.BlockSpec((1,) + shape, lambda b: (b, 0, 0))
    row = jax.ShapeDtypeStruct((batch, 1, columns), F32)
    if last:
        out_specs = [each(head, columns), each(1, columns), each(deep, columns)]
        out_shape = [jax.ShapeDtypeStruct((batch, head, columns), F32), row]
        out_shape += [jax.ShapeDtypeStruct(queries.shape, BF16)]
    else:
        out_specs = [each(1, columns), each(tall, columns)]
        out_shape = [row, jax.ShapeDtypeStruct((batch, tall, columns), F32)]
    return pl.pallas_call(
        functools.partial(
            attend_kernel, base=base, chunks=len(chunks), first=state is None, last=last, part=part
        ),
        grid=(batch,),
        in_specs=[scalars(), each(deep, columns)]
        + [each(*chunk.shape[1:]) for chunk in chunks]
        + ([] if state is None else [each(1, columns), each(tall, columns)]),
        out_specs=out_specs,
        out_shape=out_shape,
        scratch_shapes=[pltpu.VMEM((1, columns), F32), pltpu.VMEM((tall, columns), F32)],
        compiler_params=params(63),
        cost_estimate=cost(7, 1),
        name="attend",
    )(table, queries, *chunks, *([] if state is None else state))


def attend_back_kernel(*refs, base, sends, keeps, first, part):
    refs = list(refs)
    chunks = sends + keeps
    tab_ref, q_ref, scaled_ref, dw_ref = refs[:4]
    kv_refs = refs[4 : 4 + chunks]
    rest = refs[4 + chunks :]
    if first:
        before = None
    else:
        before, rest = rest[0], rest[1:]
    dq_ref, rest = rest[0], rest[1:]
    targets = [rest[0].at[index, 0] for index in range(sends)]
    targets += [ref.at[0] for ref in rest[len(rest) - keeps :]]
    columns = q_ref.shape[2]
    head = q_ref.shape[1] // 4
    length = tab_ref[pl.program_id(0)]
    dq_ref[0] = jnp.zeros((head, columns), F32) if first else before[0]
    parts = [slice(at, at + part) for at in range(0, columns, part)]
    for index, kv_ref in enumerate(kv_refs):
        count = length - tab_ref[base + index]
        target = targets[index]

        @pl.when(count > 0)
        def _(kv_ref=kv_ref, count=count, target=target):
            block = kv_ref[0].astype(F32)
            keys = spread_keys(block, count)
            lane = lax.broadcasted_iota(jnp.int32, block.shape, 1)
            values = jnp.where(lane < head, jnp.where(lane < 3, 1.0, 0.0), block).astype(BF16)
            keys_t = block.T[:head].astype(BF16)

            def products(cols):
                return dot(keys, q_ref[0, :, cols]), dot(values, dw_ref[0, :, cols])

            d_keys = jnp.zeros((head, block.shape[0]), F32)
            d_values = jnp.zeros((head, block.shape[0]), F32)
            ahead = products(parts[0])
            for p, cols in enumerate(parts):
                scores, d_expo = ahead
                if p + 1 < len(parts):
                    ahead = products(parts[p + 1])
                expo = jnp.exp2(scores)
                d_scores = (expo * d_expo).astype(BF16)
                dq_ref[0, :, cols] += dot(keys_t, d_scores)
                d_keys = d_keys + dot(scaled_ref[0, :, cols], d_scores, NT)
                d_values = d_values + dot(dw_ref[0, head:, cols], expo.astype(BF16), NT)
            target[:head, :] = d_keys.astype(BF16)
            target[head:, :] = d_values.astype(BF16)

        @pl.when(count <= 0)
        def _(target=target):
            target[...] = jnp.zeros(target.shape, BF16)


def attend_back(table, base, queries, scaled, d_weighted, sends, keeps, d_query, part=256):
    batch, deep, columns = queries.shape
    head, pair = deep // 4, deep // 2
    chunks = sends + keeps
    size = chunks[0].shape[1]
    each = lambda *shape: pl.BlockSpec((1,) + shape, lambda b: (b, 0, 0))
    stack = pl.BlockSpec((len(sends), 1, pair, size), lambda b: (0, b, 0, 0))
    stacked = [jax.ShapeDtypeStruct((len(sends), batch, pair, size), BF16)] if sends else []
    outs = pl.pallas_call(
        functools.partial(
            attend_back_kernel,
            base=base,
            sends=len(sends),
            keeps=len(keeps),
            first=d_query is None,
            part=part,
        ),
        grid=(batch,),
        in_specs=[
            scalars(),
            each(deep, columns),
            each(head, columns),
            each(pair, columns),
        ]
        + [each(size, pair)] * len(chunks)
        + ([] if d_query is None else [each(head, columns)]),
        out_specs=[each(head, columns)] + [stack] * len(stacked) + [each(pair, size)] * len(keeps),
        out_shape=[jax.ShapeDtypeStruct((batch, head, columns), F32)]
        + stacked
        + [jax.ShapeDtypeStruct((batch, pair, size), BF16)] * len(keeps),
        compiler_params=params(),
        cost_estimate=cost(8, 2),
        name="attend_back",
    )(
        table,
        queries,
        scaled,
        d_weighted,
        *chunks,
        *([] if d_query is None else [d_query]),
    )
    return outs[0], outs[1] if sends else None, outs[len(outs) - len(keeps) :]


def middle_kernel(
    len_ref,
    tok_ref,
    cot_ref,
    exp_ref,
    att_ref,
    gat_ref,
    sum_ref,
    gain_ref,
    wo_in_ref,
    up_ref,
    down_ref,
    out_ref,
    dmid_ref,
    dw_ref,
    dlog_ref,
    keep_ref,
    send_ref,
    gout_ref,
    ggain_ref,
    act_ref,
    din_ref,
    hid_ref,
    dres_ref,
    low_ref,
    spread_ref,
    wo_ref,
    *,
    batch,
    experts,
    chunk,
):
    step = pl.program_id(0)
    _, shard, width = tok_ref.shape
    hidden_units = up_ref.shape[1]
    choices = exp_ref.shape[1]

    @pl.when(step == 0)
    def _():
        wo_ref[...] = wo_in_ref[...].astype(BF16)

    @pl.when(step < batch)
    def _():
        rows = pl.ds(pl.multiple_of(step * shard, shard), shard)
        length = len_ref[step]
        offset = len_ref[batch]
        chosen = exp_ref[0]
        each = [slice(j * shard, (j + 1) * shard) for j in range(choices)]
        which = [chosen[j : j + 1, :] for j in range(choices)]
        gating = [gat_ref[0, :, cols] for cols in each]
        attended = [att_ref[0, :, cols] for cols in each]
        spread = place_experts(which, [g * a for g, a in zip(gating, attended)], experts).astype(BF16)
        spread_ref[:, rows] = spread
        middle = tok_ref[0].astype(F32) + dot(spread, wo_ref[...], TN)
        normed, inv_std = normalize(middle)
        gain = gain_ref[1:2, :]
        hidden = (normed * gain).astype(BF16)
        hid_ref[rows, :] = hidden
        position = offset + lax.broadcasted_iota(jnp.int32, (shard, width), 0)
        d_result = jnp.where(position < length, cot_ref[0].astype(F32), 0.0)
        d_result_low = d_result.astype(BF16)
        dres_ref[rows, :] = d_result_low
        result = middle
        d_hidden = jnp.zeros((shard, width), F32)
        for c in range(hidden_units // chunk):
            cols = slice(c * chunk, (c + 1) * chunk)
            inner = dot(hidden, up_ref[:, cols])
            square = inner * inner
            half = 0.5 * jnp.tanh(inner * (GELU_A + (GELU_A * GELU_B) * square)) + 0.5
            activated = (inner * half).astype(BF16)
            slope = half + (2.0 * inner) * (half - half * half) * (
                GELU_A + (3.0 * GELU_A * GELU_B) * square
            )
            act_ref[rows, cols] = activated
            result = result + dot(activated, down_ref[cols, :])
            d_inner = (dot(d_result_low, down_ref[cols, :], NT) * slope).astype(BF16)
            din_ref[rows, cols] = d_inner
            d_hidden = d_hidden + dot(d_inner, up_ref[:, cols], NT)
        out_ref[0] = result.astype(BF16)
        own_gain = jnp.sum(normed * d_hidden, axis=0, keepdims=True)

        @pl.when(step == 0)
        def _():
            ggain_ref[...] = own_gain

        @pl.when(step > 0)
        def _():
            ggain_ref[...] += own_gain

        d_middle = d_result + norm_back(normed, inv_std, d_hidden * gain)
        dmid_ref[0] = d_middle
        d_middle_low = d_middle.astype(BF16)
        low_ref[rows, :] = d_middle_low
        d_spread = dot(wo_ref[...], d_middle_low, NT)
        d_gating = []
        for j in range(choices):
            selected = pick_expert(which[j], d_spread, experts)
            d_gating.append(jnp.sum(selected * attended[j], axis=0, keepdims=True))
            share = 1.0 / sum_ref[0, :, each[j]]
            d_weighted = selected * (gating[j] * share)
            d_total = split_rows(-(gating[j] * d_gating[j]) * share, d_weighted.shape[0])
            dw_ref[0, :, each[j]] = jnp.concatenate([d_total, d_weighted], axis=0).astype(BF16)
        mixed = functools.reduce(jnp.add, [g * d for g, d in zip(gating, d_gating)])
        expert_row = lax.broadcasted_iota(jnp.int32, (experts, shard), 0)
        d_logits = jnp.zeros((experts, shard), F32)
        for j in range(choices):
            d_logits = d_logits + jnp.where(expert_row == which[j], gating[j] * (d_gating[j] - mixed), 0.0)
        dlog_ref[0] = d_logits.astype(BF16)

    @pl.when(step >= batch)
    def _():
        late = keep_ref.shape[1]
        cols = pl.ds(pl.multiple_of((step - batch) * late, late), late)
        grad_up = dot(hid_ref[...], din_ref[:, cols], TN)
        grad_down = dot(dres_ref[...], act_ref[:, cols], TN)
        first = len_ref[batch + 1] == 0
        keep_ref[...] = jnp.where(first, grad_up, grad_down).astype(BF16)
        send_ref[...] = jnp.where(first, grad_down, grad_up).astype(BF16)

    @pl.when(step == batch)
    def _():
        gout_ref[...] = dot(spread_ref[...], low_ref[...]).astype(BF16)


def middle(limits, tokens, cotangent, chosen, attended, gating, row_sum, gains, wo, up, down, experts):
    batch, shard, width = tokens.shape
    _, head, columns = attended.shape
    choices = chosen.shape[1]
    hidden_units = up.shape[1]
    chunk = 512
    parts = hidden_units // chunk
    full = lambda *shape: pl.BlockSpec(shape, lambda i: (0,) * len(shape))
    each = lambda *shape: pl.BlockSpec((1,) + shape, lambda i: (jnp.minimum(i, batch - 1), 0, 0))
    once = lambda *shape: pl.BlockSpec(
        shape, lambda i: (0,) * len(shape), pipeline_mode=pl.Buffered(1)
    )
    late = lambda i: jnp.maximum(i - batch, 0)
    spread_rows = wo.shape[0]
    total = batch * shard
    return pl.pallas_call(
        functools.partial(middle_kernel, batch=batch, experts=experts, chunk=chunk),
        grid=(batch + parts,),
        in_specs=[
            scalars(),
            each(shard, width),
            each(shard, width),
            each(choices, shard),
            each(head, columns),
            each(1, columns),
            each(1, columns),
            full(*gains.shape),
            once(*wo.shape),
            once(*up.shape),
            once(*down.shape),
        ],
        out_specs=[
            each(shard, width),
            each(shard, width),
            each(2 * head, columns),
            each(experts, shard),
            pl.BlockSpec((width, chunk), lambda i: (0, late(i))),
            pl.BlockSpec((width, chunk), lambda i: (0, late(i))),
            full(*wo.shape),
            full(1, width),
        ],
        out_shape=[
            jax.ShapeDtypeStruct((batch, shard, width), BF16),
            jax.ShapeDtypeStruct((batch, shard, width), F32),
            jax.ShapeDtypeStruct((batch, 2 * head, columns), BF16),
            jax.ShapeDtypeStruct((batch, experts, shard), BF16),
            jax.ShapeDtypeStruct((width, hidden_units), BF16),
            jax.ShapeDtypeStruct((width, hidden_units), BF16),
            jax.ShapeDtypeStruct(wo.shape, BF16),
            jax.ShapeDtypeStruct((1, width), F32),
        ],
        scratch_shapes=[
            pltpu.VMEM((total, hidden_units), BF16),
            pltpu.VMEM((total, hidden_units), BF16),
            pltpu.VMEM((total, width), BF16),
            pltpu.VMEM((total, width), BF16),
            pltpu.VMEM((total, width), BF16),
            pltpu.VMEM((spread_rows, total), BF16),
            pltpu.VMEM(wo.shape, BF16),
        ],
        compiler_params=params(),
        cost_estimate=cost(28, 20),
        name="middle",
    )(limits, tokens, cotangent, chosen, attended, gating, row_sum, gains, wo, up, down)


def query_grad_kernel(hid_ref, dq_ref, exp_ref, dlog_ref, wq_ref, wr_ref, gq_ref, gr_ref, dhid_ref, sum_ref):
    experts = wr_ref.shape[0]
    shard = hid_ref.shape[1]
    head = dq_ref.shape[1]
    choices = exp_ref.shape[1]
    step = pl.program_id(0)
    hidden = hid_ref[0]
    chosen = exp_ref[0]
    which = [chosen[j : j + 1, :] for j in range(choices)]
    blocks = [dq_ref[0, :, j * shard : (j + 1) * shard] * head**-0.5 for j in range(choices)]
    d_query_all = place_experts(which, blocks, experts).astype(BF16)
    d_logits = dlog_ref[0]
    own_query = dot(d_query_all, hidden)
    own_router = dot(d_logits, hidden)

    @pl.when(step == 0)
    def _():
        sum_ref[...] = own_query
        gr_ref[...] = own_router

    @pl.when(step > 0)
    def _():
        sum_ref[...] += own_query
        gr_ref[...] += own_router

    gq_ref[...] = sum_ref[...].astype(BF16)

    dhid_ref[0] = dot(d_query_all, wq_ref[...].astype(BF16), TN) + dot(
        d_logits, wr_ref[...].astype(BF16), TN
    )


def query_grad(hidden, d_query, chosen, d_logits, wq, wr):
    batch, shard, width = hidden.shape
    _, head, columns = d_query.shape
    choices = chosen.shape[1]
    experts = wr.shape[0]
    full = lambda *shape: pl.BlockSpec(shape, lambda b: (0,) * len(shape))
    each = lambda *shape: pl.BlockSpec((1,) + shape, lambda b: (b, 0, 0))
    return pl.pallas_call(
        query_grad_kernel,
        grid=(batch,),
        in_specs=[
            each(shard, width),
            each(head, columns),
            each(choices, shard),
            each(experts, shard),
            full(*wq.shape),
            full(*wr.shape),
        ],
        out_specs=[full(*wq.shape), full(*wr.shape), each(shard, width)],
        out_shape=[
            jax.ShapeDtypeStruct(wq.shape, BF16),
            jax.ShapeDtypeStruct(wr.shape, F32),
            jax.ShapeDtypeStruct((batch, shard, width), F32),
        ],
        scratch_shapes=[pltpu.VMEM(wq.shape, F32)],
        compiler_params=params(),
        cost_estimate=cost(2, 6),
        name="query_grad",
    )(hidden, d_query, chosen, d_logits, wq, wr)


def input_grad_kernel(
    tok_ref,
    hid_ref,
    dpair_ref,
    dhid_ref,
    dmid_ref,
    gain_ref,
    wkv_ref,
    query_ref,
    out_ref,
    router_ref,
    two_ref,
    gin_ref,
    tail_ref,
    gkv_ref,
    one_ref,
):
    step = pl.program_id(0)
    normed, inv_std = normalize(tok_ref[0].astype(F32))
    d_pair = dpair_ref[0]
    d_hidden = dhid_ref[0] + dot(d_pair, wkv_ref[...].astype(BF16), TN)
    own_pair = dot(d_pair, hid_ref[0])
    own_gain = jnp.sum(normed * d_hidden, axis=0, keepdims=True)

    @pl.when(step == 0)
    def _():
        gkv_ref[...] = own_pair
        one_ref[...] = own_gain

    @pl.when(step > 0)
    def _():
        gkv_ref[...] += own_pair
        one_ref[...] += own_gain

    d_inputs = dmid_ref[0] + norm_back(normed, inv_std, d_hidden * gain_ref[0:1, :])
    gin_ref[0] = d_inputs.astype(BF16)
    query_rows, width = query_ref.shape
    head_rows = query_rows + out_ref.shape[0]
    used = head_rows + gkv_ref.shape[0] + router_ref.shape[0] + 2
    blank = jnp.zeros((tail_ref.shape[0] - used, width), F32)
    small = [gkv_ref[...], router_ref[...], one_ref[...], two_ref[...], blank]
    tail_ref[:query_rows, :] = query_ref[...]
    tail_ref[query_rows:head_rows, :] = out_ref[...]
    tail_ref[head_rows:, :] = jnp.concatenate(small, axis=0).astype(BF16)


def input_grad(
    tokens, hidden, d_pair, d_hidden, d_middle, gains, wkv, grad_query, grad_out, grad_router, grad_gain_two
):
    batch, shard, width = tokens.shape
    pair = wkv.shape[0]
    rows = -(-(grad_query.shape[0] + grad_out.shape[0] + pair + grad_router.shape[0] + 2) // 64) * 64
    full = lambda *shape: pl.BlockSpec(shape, lambda b: (0,) * len(shape))
    each = lambda *shape: pl.BlockSpec((1,) + shape, lambda b: (b, 0, 0))
    return pl.pallas_call(
        input_grad_kernel,
        grid=(batch,),
        in_specs=[
            each(shard, width),
            each(shard, width),
            each(pair, shard),
            each(shard, width),
            each(shard, width),
            full(*gains.shape),
            full(*wkv.shape),
            full(*grad_query.shape),
            full(*grad_out.shape),
            full(*grad_router.shape),
            full(*grad_gain_two.shape),
        ],
        out_specs=[each(shard, width), full(rows, width)],
        out_shape=[
            jax.ShapeDtypeStruct((batch, shard, width), BF16),
            jax.ShapeDtypeStruct((rows, width), BF16),
        ],
        scratch_shapes=[pltpu.VMEM(wkv.shape, F32), pltpu.VMEM((1, width), F32)],
        compiler_params=params(),
        cost_estimate=cost(2, 9),
        name="input_grad",
    )(tokens, hidden, d_pair, d_hidden, d_middle, gains, wkv, grad_query, grad_out, grad_router, grad_gain_two)


def square_fine(matrix):
    high = matrix.astype(BF16)
    rest = (matrix - high.astype(F32)).astype(BF16)
    cross = dot(high, rest)
    return dot(high, high) + (cross + cross.T)


def mirrored(left, bottom):
    half = bottom.shape[0]
    right = jnp.concatenate([left[half:].T, bottom], axis=0)
    return jnp.concatenate([left, right], axis=1)


def gram_of(low):
    half = low.shape[0] // 2
    return mirrored(dot(low, low[:half], NT), dot(low[half:], low[half:], NT))


def square_of(gram):
    half = gram.shape[0] // 2
    high = gram.astype(BF16)
    rest = (gram - high.astype(F32)).astype(BF16)
    cross = dot(high, rest)
    return mirrored(dot(high, high[:, :half]), dot(high[half:], high[:, half:])) + (cross + cross.T)


def muon_kernel(core_ref, up_ref, down_ref, grad_in_ref, solved_ref, x_ref, low_ref, turn_ref, grad_ref, sems):
    rows, cols = x_ref.shape
    fetch = pltpu.make_async_copy(grad_in_ref, grad_ref, sems.at[0])
    fetch.start()

    @pl.when(core_ref[0] == 0)
    def _():
        copy = pltpu.make_async_copy(up_ref, x_ref, sems.at[1])
        copy.start()
        copy.wait()

    @pl.when(core_ref[0] != 0)
    def _():
        pieces = range(0, cols, rows)
        copies = [
            pltpu.make_async_copy(
                down_ref.at[pl.ds(at, rows), :], turn_ref.at[pl.ds(at, rows), :], sems.at[2 + index]
            )
            for index, at in enumerate(pieces)
        ]
        for copy in copies:
            copy.start()
        for copy, at in zip(copies, pieces):
            copy.wait()
            x_ref[:, at : at + rows] = turn_ref[at : at + rows, :].T

    fetch.wait()

    renewed = MOMENT_DECAY * x_ref[...] + grad_ref[:, :cols].astype(F32)
    inverse = 1.0 / (jnp.sqrt(jnp.sum(renewed * renewed)) + 1e-07)
    first = renewed * inverse
    x_ref[...] = first
    low_ref[...] = first.astype(BF16)

    def iterate(_, carry):
        low = low_ref[...]
        gram = gram_of(low)
        poly = (NEWTON_B * gram + NEWTON_C * square_of(gram)).astype(BF16)
        following = NEWTON_A * x_ref[...] + dot(poly, low)
        x_ref[...] = following
        low_ref[...] = following.astype(BF16)
        return carry

    lax.fori_loop(0, 5, iterate, 0)
    solved_ref[...] = low_ref[...]


def muon(core_ref, up_mom, down_mom, grad):
    anywhere = pl.BlockSpec(memory_space=pl.ANY)
    return pl.pallas_call(
        muon_kernel,
        in_specs=[scalars(), anywhere, anywhere, anywhere],
        out_specs=whole(),
        out_shape=jax.ShapeDtypeStruct(up_mom.shape, BF16),
        scratch_shapes=[
            pltpu.VMEM(up_mom.shape, F32),
            pltpu.VMEM(up_mom.shape, BF16),
            pltpu.VMEM(down_mom.shape, F32),
            pltpu.VMEM(grad.shape, BF16),
            pltpu.SemaphoreType.DMA((2 + max(down_mom.shape) // min(down_mom.shape),)),
        ],
        compiler_params=params(),
        cost_estimate=cost(25, 8),
        name="muon",
    )(core_ref, up_mom, down_mom, grad)


def prepare_kernel(up_ref, down_ref, up_low_ref, down_low_ref, up_square_ref, down_square_ref):
    for ref, low_ref, square_ref in (
        (up_ref, up_low_ref, up_square_ref),
        (down_ref, down_low_ref, down_square_ref),
    ):
        weight = ref[...]
        low_ref[...] = weight.astype(BF16)
        total = jnp.sum(jnp.sum(weight * weight, axis=0, keepdims=True), axis=1, keepdims=True)

        @pl.when(pl.program_id(0) == 0)
        def _(square_ref=square_ref, total=total):
            square_ref[...] = total

        @pl.when(pl.program_id(0) > 0)
        def _(square_ref=square_ref, total=total):
            square_ref[...] += total


def prepare(up, down, steps=4):
    rows, cols = up.shape
    one = pl.BlockSpec((1, 1), lambda i: (0, 0))
    flat = pl.BlockSpec((rows // steps, cols), lambda i: (i, 0))
    turned = pl.BlockSpec((cols // steps, rows), lambda i: (i, 0))
    return pl.pallas_call(
        prepare_kernel,
        grid=(steps,),
        in_specs=[flat, turned],
        out_specs=[flat, turned, one, one],
        out_shape=[
            jax.ShapeDtypeStruct(up.shape, BF16),
            jax.ShapeDtypeStruct(down.shape, BF16),
            jax.ShapeDtypeStruct((1, 1), F32),
            jax.ShapeDtypeStruct((1, 1), F32),
        ],
        compiler_params=params(),
        cost_estimate=cost(1, 12),
        name="prepare",
    )(up, down)


def blend_block(first, square_refs, refs, rank):
    up_ref, down_ref, own_rows, other_rows, own_cols, other_cols, up_out, down_out = refs
    for ref, out, one, two, turn in (
        (up_ref, up_out, own_rows, other_rows, False),
        (down_ref, down_out, other_cols, own_cols, True),
    ):
        change = jnp.where(first, one[...].astype(F32), two[...].astype(F32))
        change = change.T if turn else change
        if square_refs:
            step = jnp.sqrt(square_refs[1 if turn else 0][...]) * (STEP_RATE / math.sqrt(rank))
            out[...] = ref[...] - step * change
        else:
            out[...] = MOMENT_DECAY * ref[...] + change


def blend_specs(up, down, steps):
    rows, cols = up.shape
    flat = pl.BlockSpec((rows // steps, cols), lambda i, core: (i, 0))
    turned = pl.BlockSpec((cols // steps, rows), lambda i, core: (i, 0))

    def wanted(i, core, turn):
        return jnp.where(core[0] == turn, i, 0)

    row_specs = [
        pl.BlockSpec((rows // steps, cols), lambda i, core, turn=turn: (wanted(i, core, turn), 0)) for turn in (0, 1)
    ]
    col_specs = [
        pl.BlockSpec((rows, cols // steps), lambda i, core, turn=turn: (0, wanted(i, core, turn))) for turn in (1, 0)
    ]
    return [flat, turned] + row_specs + col_specs, [flat, turned]


def by_block(values, sizes, finish):
    pieces = []
    at = 0
    for size in sizes:
        piece = values[at : at + size]
        total = jnp.sum(jnp.sum(piece * piece, axis=1, keepdims=True), axis=0, keepdims=True)
        pieces.append(jnp.broadcast_to(finish(total, size), (size, 1)))
        at += size
    return jnp.concatenate(pieces, axis=0)


def block_ids(sizes, axis):
    index = lax.broadcasted_iota(jnp.int32, (sum(sizes), sum(sizes)), axis)
    ids = jnp.zeros(index.shape, jnp.int32)
    at = 0
    for size in sizes[:-1]:
        at += size
        ids = ids + (index >= at).astype(jnp.int32)
    return ids


def solve_packs(step, sizes, x_ref, renew, weights_of, store):
    @pl.when(step == 0)
    def _():
        for index, moment in enumerate(renew()):
            x_ref[index] = moment * by_block(moment, sizes, lambda total, _: 1.0 / (jnp.sqrt(total) + 1e-07))

    @pl.when((step >= 1) & (step <= 5))
    def _():
        same = block_ids(sizes, 0) == block_ids(sizes, 1)
        matrices = [x_ref[index] for index in range(x_ref.shape[0])]
        lows = [matrix.astype(BF16) for matrix in matrices]
        grams = [jnp.where(same, dot(low, low, NT), 0.0) for low in lows]
        squares = [square_fine(gram) for gram in grams]
        polys = [(NEWTON_B * g + NEWTON_C * q).astype(BF16) for g, q in zip(grams, squares)]
        for index, (matrix, poly, low) in enumerate(zip(matrices, polys, lows)):
            x_ref[index] = NEWTON_A * matrix + dot(poly, low)

    @pl.when(step == 6)
    def _():
        fresh = []
        for index, (weight, ranks) in enumerate(weights_of()):
            factors = iter([STEP_RATE / math.sqrt(min(weight.shape[1], rank)) for rank in ranks])
            scale = by_block(weight, sizes, lambda total, _: jnp.sqrt(total) * next(factors))
            fresh.append(weight - scale * x_ref[index])
        store(fresh)


STEPS = 8


def renew_kernel(core_ref, *refs):
    blend_block(core_ref[0] == 0, [], refs, min(refs[2].shape))


def renew(core_ref, up_mom, down_mom, own, other):
    ins, outs = blend_specs(up_mom, down_mom, STEPS)
    return pl.pallas_call(
        renew_kernel,
        grid_spec=pltpu.PrefetchScalarGridSpec(num_scalar_prefetch=1, grid=(STEPS,), in_specs=ins, out_specs=outs),
        out_shape=[jax.ShapeDtypeStruct(array.shape, F32) for array in (up_mom, down_mom)],
        compiler_params=params(),
        cost_estimate=cost(1, 20),
        name="renew",
    )(core_ref, up_mom, down_mom, own, other, own, other)


def move_kernel(core_ref, *refs, head, gain_rate, rank):
    square_refs = refs[:2]
    blend_refs = refs[2:8] + refs[19:21]
    wq_ref, wo_ref, wkv_ref, wr_ref, gain_ref, mq_ref, mo_ref, mkv_ref, mr_ref, mgain_ref, tail_ref = refs[8:19]
    wq_out, wo_out, wkv_out, wr_out, gain_out, mq_out, mo_out, mkv_out, mr_out, mgain_out, x_ref = refs[21:]
    sizes = (head,) * 4
    rows = sum(sizes)
    query_rows, pair, experts = wq_ref.shape[0], wkv_ref.shape[0], wr_ref.shape[0]
    head_rows = query_rows + wo_ref.shape[0]
    places = [
        (weight, moment, target, slice(at, at + rows))
        for weight, moment, target in ((wq_ref, mq_out, wq_out), (wo_ref, mo_out, wo_out))
        for at in range(0, weight.shape[0], rows)
    ]
    blank = jnp.zeros((rows - pair - experts, wkv_ref.shape[1]), F32)

    def renewed():
        mq_out[...] = MOMENT_DECAY * mq_ref[...] + tail_ref[:query_rows, :].astype(F32)
        mo_out[...] = MOMENT_DECAY * mo_ref[...] + tail_ref[query_rows:head_rows, :].astype(F32)
        small = tail_ref[head_rows:, :].astype(F32)
        mkv_out[...] = MOMENT_DECAY * mkv_ref[...] + small[:pair]
        mr_out[...] = MOMENT_DECAY * mr_ref[...] + small[pair : pair + experts]
        gain_moment = MOMENT_DECAY * mgain_ref[...] + small[pair + experts : pair + experts + 2]
        mgain_out[...] = gain_moment
        gain_out[...] = gain_ref[...] - gain_rate * gain_moment
        last = jnp.concatenate([mkv_out[...], mr_out[...], blank], axis=0)
        return [moment[at, :] for _, moment, _, at in places] + [last]

    def weights_of():
        last = jnp.concatenate([wkv_ref[...], wr_ref[...], blank], axis=0)
        return [(weight[at, :], sizes) for weight, _, _, at in places] + [(last, (head, head, experts, head))]

    def store(fresh):
        for (_, _, target, at), value in zip(places, fresh):
            target[at, :] = value
        wkv_out[...] = fresh[-1][:pair]
        wr_out[...] = fresh[-1][pair : pair + experts]

    solve_packs(pl.program_id(0), sizes, x_ref, renewed, weights_of, store)
    blend_block(core_ref[0] == 0, square_refs, blend_refs, rank)


def move_and_tail(core_ref, squares, up, down, own, other, weights, moments, tail, head, gain_rate):
    ins, outs = blend_specs(up, down, STEPS)
    one = pl.BlockSpec((1, 1), lambda i, core: (0, 0))
    full = lambda array: pl.BlockSpec(array.shape, lambda i, core: (0, 0))
    arrays = weights + moments
    rows = 4 * head
    return pl.pallas_call(
        functools.partial(move_kernel, head=head, gain_rate=gain_rate, rank=min(up.shape)),
        grid_spec=pltpu.PrefetchScalarGridSpec(
            num_scalar_prefetch=1,
            grid=(STEPS,),
            in_specs=[one, one] + ins + [full(array) for array in arrays + [tail]],
            out_specs=outs + [full(array) for array in arrays],
            scratch_shapes=[pltpu.VMEM(((weights[0].shape[0] + weights[1].shape[0]) // rows + 1, rows, up.shape[0]), F32)],
        ),
        out_shape=[jax.ShapeDtypeStruct(array.shape, F32) for array in [up, down] + arrays],
        compiler_params=params(),
        cost_estimate=cost(1, 20),
        name="move_and_tail",
    )(core_ref, *squares, up, down, own, other, own, other, *arrays, tail)


def after(*values):
    return lax.optimization_barrier(values)


class Sums:
    def __init__(self):
        self.planes, self.lines = lax.axis_size("dp"), lax.axis_size("seq")
        plane_bits = range(self.planes.bit_length() - 1)
        self.orders = [[(1 << bit, 0) for bit in bits] for bits in (plane_bits, reversed(plane_bits))]
        self.plane, self.line = lax.axis_index("dp"), lax.axis_index("seq")
        self.table = None

    def send(self, value, pairs):
        if self.table is not None:
            value, self.table = after(value, self.table)
        return lax.ppermute(value, ("dp", "seq"), pairs)

    def exchange(self, value, flips):
        pairs = []
        for plane in range(self.planes):
            for line in range(self.lines):
                flip = flips[line % 2]
                pairs.append((plane * self.lines + line, (plane ^ flip[0]) * self.lines + (line ^ flip[1])))
        return self.send(value, pairs)

    def stages(self):
        return list(zip(*self.orders))

    def upper(self, flips):
        sides = [((self.plane & flip[0]) | (self.line & flip[1])) != 0 for flip in flips]
        return jnp.where(self.line % 2 == 0, sides[0], sides[1])

    def sibling(self, value):
        return self.exchange(value, ((0, 1), (0, 1)))

    def add_up(self, *terms):
        return functools.reduce(jnp.add, [term.astype(F32) for term in terms]).astype(terms[0].dtype)

    def halve(self, rows, upper, flips):
        half = rows.shape[0] // 2
        low, high = rows[:half], rows[half:]
        return self.exchange(jnp.where(upper, low, high), flips), jnp.where(upper, high, low)

    def join(self, rows, arrived, upper):
        return jnp.concatenate([jnp.where(upper, arrived, rows), jnp.where(upper, rows, arrived)], axis=0)

    def to_chip(self, value, mask):
        return self.exchange(value, ((0, 2 * mask), (0, 2 * mask)))


def per_device(
    tokens_in,
    cotangent,
    lengths,
    experts_top,
    gains,
    router,
    query_w,
    key_value_w,
    out_w,
    up_w,
    down_w,
    gains_mom,
    router_mom,
    query_mom,
    key_value_mom,
    out_mom,
    up_mom,
    down_mom,
):
    batch_here, shard_len, width = tokens_in.shape
    experts, _, head = query_w.shape
    seq_devices = lax.axis_size("seq")
    seq_len = shard_len * seq_devices
    token_total = batch_here * lax.axis_size("dp") * seq_len

    def wide(stacked):
        return jnp.swapaxes(stacked, -1, -2).reshape(-1, width)

    def narrow(rows):
        return jnp.swapaxes(rows.reshape(-1, head, width), -1, -2)

    chosen = jnp.swapaxes(experts_top, 1, 2)
    wq, wkv, wr = wide(query_w), wide(key_value_w), router.T
    wo = out_w.reshape(-1, width)
    sums = Sums()
    place = lax.axis_index("seq").astype(jnp.int32)
    core, chip = place % 2, place // 2
    chips = seq_devices // 2
    core_ref = core[None]

    rounds = [
        [away for away in range(chips) if away.bit_count() == bits] for bits in range(chips.bit_length())
    ]
    own_turns = [[(away, core) for away in members] for members in rounds]
    sibling_turns = [[(away, 1 - core) for away in members] for members in rounds]
    forward = [own_turns[0] + sibling_turns[0]] + own_turns[1:] + [[]]
    for turn in range(1, len(rounds)):
        forward[turn + 1] = sibling_turns[turn] + forward[turn + 1]
    last = len(rounds)
    sends_of = [rounds[last - 1 - call] for call in range(last)] + [[]]
    sends_of[last - 2], sends_of[last - 1] = sends_of[last - 2] + rounds[0], []
    keeps_of = [[]] + rounds[::-1]
    backward = [
        [(away, 1 - core) for away in theirs] + [(away, core) for away in ours]
        for theirs, ours in zip(sends_of, keeps_of)
    ]
    bases, starts = [], []
    for group in forward + backward:
        bases.append(batch_here + 2 + len(starts))
        starts += [(2 * (chip ^ away) + which) * shard_len for away, which in group]
    table = jnp.concatenate([lengths, jnp.stack([place * shard_len, core] + starts)])

    hidden, key_value, queries, scaled, gating = project(tokens_in, chosen, gains, wq, wkv, wr)
    sums.table = table
    blocks, siblings = {0: key_value}, {0: sums.sibling(key_value)}
    incoming = [sums.to_chip(key_value, away) for away in rounds[1]]
    state = attend(sums.table, bases[0], queries, [blocks[0], siblings[0]], None, False)
    up_late, state = after(up_w, state)
    up_low, down_low, *squares = prepare(up_late, down_w)
    squares, sums.table = after(squares, sums.table)
    for turn in range(1, len(rounds) + 1):
        group = []
        if turn > 1:
            group += [siblings[away] for away in rounds[turn - 1]]
        if turn < len(rounds):
            incoming, state, sums.table = after(incoming, state, sums.table)
            blocks.update(zip(rounds[turn], incoming))
            group += incoming
            incoming = [
                sums.to_chip(blocks[away & (away - 1)], away & -away)
                for away in (rounds[turn + 1] if turn + 1 < len(rounds) else [])
            ]
            siblings.update((away, sums.sibling(blocks[away])) for away in rounds[turn])
        state = attend(sums.table, bases[turn], queries, group, state, turn == len(rounds))
    attended, row_sum, back_queries = state
    (
        layer_out,
        d_middle,
        d_weighted,
        d_logits,
        keep,
        send,
        grad_out,
        grad_gain_two,
    ) = middle(
        sums.table,
        tokens_in,
        cotangent,
        chosen,
        attended,
        gating,
        row_sum,
        gains,
        wo,
        up_low,
        down_low,
        experts,
    )
    stages = sums.stages()

    def halving(flips):
        def step(arrived):
            return list(sums.halve(sums.add_up(*arrived), sums.upper(flips), flips))

        return step

    def doubling(flips):
        def step(arrived):
            return [arrived[0], sums.exchange(arrived[0], flips)]

        return step

    def joined(flips, step):
        return lambda arrived: step([sums.join(*arrived, sums.upper(flips))])

    stages += [((0, 2 << bit), (0, 2 << bit)) for bit in range(chips.bit_length() - 1)]
    back = stages[::-1]
    ffn_steps = [halving(flips) for flips in stages]
    ffn_steps.append(lambda arrived: doubling(back[0])([sums.add_up(*arrived)]))
    for earlier, flips in zip(back, back[1:]):
        ffn_steps.append(joined(earlier, doubling(flips)))

    ffn = [sums.sibling(send), keep]
    d_query, crossing, arrived = None, {}, {}
    grown = {away: [] for away in range(chips)}
    for call in range(last + 1):
        theirs, ours = sends_of[call], keeps_of[call]
        d_query, d_send, d_keeps = attend_back(
            sums.table,
            bases[last + 1 + call],
            back_queries,
            scaled,
            d_weighted,
            [siblings[away] for away in theirs],
            [blocks[away] for away in ours],
            d_query,
        )
        if call == last:
            break
        d_query, d_send, ffn, crossing, grown = after(d_query, d_send, ffn, crossing, grown)
        if len(ffn_steps) > 5:
            ffn = ffn_steps.pop(0)(ffn)
        arrived.update(crossing)
        crossing = {}
        if theirs:
            exchanged = sums.sibling(d_send)
            crossing = {away: exchanged[i] for i, away in enumerate(theirs)}
        for away, d_keep in zip(ours, d_keeps):
            total = sums.add_up(d_keep, arrived[away], *grown[away])
            grown[away ^ (away & -away)].append(sums.to_chip(total, away & -away))

    sums.table = core_ref
    ffn, d_query = after(ffn, d_query)
    while len(ffn_steps) > 4:
        ffn = ffn_steps.pop(0)(ffn)
    hidden, sums.table = after(hidden, sums.table)
    grad_query, grad_router, d_hidden = query_grad(hidden, d_query, chosen, d_logits, wq, wr)
    sides = [d_keeps[0], arrived[0], *grown[0]]
    ffn, sides, grad_query = after(ffn, sides, grad_query)
    ffn = ffn_steps.pop(0)(ffn)
    d_hidden, sides, sums.table = after(d_hidden, sides, sums.table)
    input_gradient, tail = input_grad(
        tokens_in,
        hidden,
        sums.add_up(*sides),
        d_hidden,
        d_middle,
        gains,
        wkv,
        grad_query,
        grad_out,
        grad_router,
        grad_gain_two,
    )
    second = core == 1
    ffn, tail = after(ffn, tail)
    ffn = ffn_steps.pop(0)(ffn)
    plane_stages = sums.stages()
    plane_back = plane_stages[::-1]
    tail_steps = [halving(flips) for flips in plane_stages]
    tail_steps += [lambda arrived, flips=flips: doubling(flips)([sums.add_up(*arrived)]) for flips in back[::-1][len(plane_back) :]]
    tail_steps.append(lambda arrived: doubling(plane_back[0])([sums.add_up(*arrived)]))
    tail_steps += [joined(earlier, doubling(flips)) for earlier, flips in zip(plane_back, plane_back[1:])]

    def tail_step(tail):
        tail, sums.table = after(tail, sums.table)
        return tail_steps.pop(0)(tail)

    tail = list(sums.halve(tail, second, ((0, 1), (0, 1))))
    ffn, sums.table = after(ffn, sums.table)
    ffn = ffn_steps.pop(0)(ffn)
    tail = tail_step(tail)
    tail = tail_step(tail)
    ffn, sums.table = after(ffn, sums.table)
    ffn = ffn_steps.pop(0)(ffn)
    while len(tail_steps) > 1:
        tail = tail_step(tail)
    ffn, sums.table = after(ffn, sums.table)
    own_ffn = sums.join(*ffn, sums.upper(back[-1]))
    other_ffn = sums.sibling(own_ffn)
    solved_ffn = muon(sums.table, up_mom, down_mom, own_ffn)
    tail, other_ffn, solved_ffn = after(tail, other_ffn, solved_ffn)
    other_solved = sums.sibling(solved_ffn)
    tail = tail_step(tail)
    up_mom_new, down_mom_new = renew(sums.table, up_mom, down_mom, own_ffn, other_ffn)
    tail, other_solved, up_mom_new = after(tail, other_solved, up_mom_new)
    tail = sums.join(*tail, sums.upper(plane_back[-1]))
    tail = sums.join(tail, sums.sibling(tail), second)
    (
        up_new,
        down_new,
        query_new,
        out_new,
        pair_new,
        router_new,
        gains_new,
        query_mom_new,
        out_mom_new,
        pair_mom_new,
        router_mom_new,
        gains_mom_new,
    ) = move_and_tail(
        sums.table,
        squares,
        up_w,
        down_w,
        solved_ffn,
        other_solved,
        [wq, wo, wkv, wr, gains],
        [wide(query_mom), out_mom.reshape(-1, width), wide(key_value_mom), router_mom.T, gains_mom],
        tail,
        head,
        GAIN_RATE / math.sqrt(token_total),
    )
    return (
        layer_out,
        input_gradient,
        gains_new,
        gains_mom_new,
        router_new.T,
        router_mom_new.T,
        narrow(query_new),
        narrow(query_mom_new),
        narrow(pair_new),
        narrow(pair_mom_new),
        out_new.reshape(out_w.shape),
        out_mom_new.reshape(out_w.shape),
        up_new,
        up_mom_new,
        down_new,
        down_mom_new,
    )


def solution(mesh):
    split = P("dp", "seq", None)
    return jax.shard_map(
        per_device,
        mesh=mesh,
        in_specs=(split, split, P("dp"), split) + (P(),) * 14,
        out_specs=(split, split) + (P(),) * 14,
        check_vma=False,
    )
```
